128 devices in a mesh: term: 8 (over x_hi, y), sector: 16 (over x_lo, z, core).
Axes of the slice: x: 4 (x_hi: 2, x_lo: 2; x = x_hi * 2 + x_lo), y: 4, z: 4, core: 2. Of those that a mesh axis runs over, the one named last changes fastest.
Arguments:
- wavefunction: bfloat16 [16, 512, 512], P('sector'), may hold values from -6 to 6
- left_ops: bfloat16 [256, 512, 512], P(('term', 'sector')), may hold values from -0.125 to 0.125
- right_ops: bfloat16 [256, 512, 512], P(('term', 'sector')), may hold values from -0.125 to 0.125
- sector_dims: int32 [16], replicated, may hold values from 128 to 512, as said below
- coupling_source: int32 [3072], P(('term', 'sector')), may hold values from 0 to 15
- coupling_target: int32 [3072], P(('term', 'sector')), may hold values from 0 to 15
- coupling_operator: int32 [3072], P(('term', 'sector')), may hold values from 0 to 1
Outputs:
- sigma_blocks: float32 [16, 512, 512], P('sector')
The draws below stay inside these ranges and needn't reach their ends.
Inputs may be any that keep to these rules, and one draw needn't show every extreme that they name: `sector_dims`: multiples of 128; at least one sector has dimension 512.
All inputs are finite; a program needn't handle non-finite values.
Results may differ from the reference program's by a relative error of at most 0.0029.
Values may be sent and summed in bfloat16 or wider, within the bound.
No kernel may reach another device: no remote copies, remote signals or barrier semaphores. Data moves between devices by JAX's collectives and lax.ppermute only.
A program may use at most 128 MiB of HBM per device.

```python
import jax
import jax.numpy as jnp
from jax import lax

BMAX = 512
QUANT = 128
OPS_DEV = 2
CPL_DEV = 24
SECTORS = 16
OPS = 256
COUPLINGS = 3072


def draw_sector_dims(key, part):
    key = jax.random.fold_in(key, 11)
    levels = jax.random.randint(key, (SECTORS,), 1, BMAX // QUANT + 1)
    chosen_spot = jax.random.randint(jax.random.fold_in(key, 1), (), 0, SECTORS)
    levels = jnp.where(jnp.arange(SECTORS) == chosen_spot, BMAX // QUANT, levels)
    return (levels * QUANT).astype(jnp.int32)


def with_ends(drawn, stream_key, low, high):
    longest = drawn.shape.index(max(drawn.shape))
    spots = []
    for shift in (0, 1):
        where = [jax.random.randint(jax.random.fold_in(stream_key, axis), (), 0, length) for axis, length in enumerate(drawn.shape)]
        where[longest] = (where[longest] + shift) % drawn.shape[longest]
        spots.append(tuple(where))
    return drawn.at[spots[0]].set(low).at[spots[1]].set(high)


def shard_levels(stream_key, shape, cuts, smallest, largest):
    factor_of, own = 1.0, jax.random.fold_in(stream_key, 6)
    for dim, shards_of in cuts:
        steps = jnp.exp(jax.random.uniform(jax.random.fold_in(own, dim), (shards_of,), jnp.float32, smallest / len(cuts), largest / len(cuts)))
        factor_of = factor_of * jnp.repeat(steps, shape[dim] // shards_of).reshape([-1 if axis == dim else 1 for axis in range(len(shape))])
    return factor_of


def normal_values(rng, dims, deviation, reach, cuts=(), held_as=jnp.bfloat16):
    drawn = deviation * jax.random.normal(rng, dims, jnp.float32)
    if cuts:
        drawn = drawn * shard_levels(rng, dims, cuts, -0.22, 0.18)
    return jnp.clip(drawn, -reach, reach).astype(held_as)


def setup_inputs(seed: int = 0) -> dict:
    splits = jax.random.split(jax.random.key(seed), 8)
    wavefunction = normal_values(splits[0], (SECTORS, BMAX, BMAX), 1.0, 6.0, ((0, 16),))
    left_ops = normal_values(splits[1], (OPS, BMAX, BMAX), (BMAX * 4) ** -0.5, 0.125, ((0, 128),))
    right_ops = normal_values(splits[2], (OPS, BMAX, BMAX), (BMAX * 4) ** -0.5, 0.125, ((0, 128),))
    sector_dims = draw_sector_dims(jax.random.fold_in(splits[7], 71), 0)
    coupling_source = with_ends(jax.random.randint(splits[4], (COUPLINGS,), 0, SECTORS), jax.random.fold_in(splits[4], 1), 0, SECTORS - 1).astype(jnp.int32)
    coupling_target = with_ends(jax.random.randint(splits[5], (COUPLINGS,), 0, SECTORS), jax.random.fold_in(splits[5], 1), 0, SECTORS - 1).astype(jnp.int32)
    coupling_operator = with_ends(jax.random.randint(splits[6], (COUPLINGS,), 0, OPS_DEV), jax.random.fold_in(splits[6], 1), 0, OPS_DEV - 1).astype(jnp.int32)
    return {"wavefunction": wavefunction, "left_ops": left_ops, "right_ops": right_ops, "sector_dims": sector_dims, "coupling_source": coupling_source, "coupling_target": coupling_target, "coupling_operator": coupling_operator}


def reference(wavefunction, left_ops, right_ops, sector_dims, coupling_source, coupling_target, coupling_operator):
    positions = jnp.arange(BMAX, dtype=jnp.int32)
    kept_rows = positions[None, :] < sector_dims[:, None]
    sector_mask = kept_rows[:, :, None] & kept_rows[:, None, :]
    masked_wave = wavefunction * sector_mask.astype(jnp.bfloat16)
    owner_index = (jnp.arange(COUPLINGS, dtype=jnp.int32) // CPL_DEV).astype(jnp.int32)
    operator_index = (owner_index * OPS_DEV + coupling_operator).astype(jnp.int32)

    def advance(blocks, coupling):
        source, target, chosen = coupling
        halfway = jnp.dot(left_ops[chosen], masked_wave[source], preferred_element_type=jnp.float32).astype(jnp.bfloat16)
        contribution = jnp.dot(halfway, right_ops[chosen], preferred_element_type=jnp.float32)
        return blocks.at[target].add(contribution), None

    start_blocks = jnp.zeros((SECTORS, BMAX, BMAX), jnp.float32)
    raw_blocks = lax.scan(advance, start_blocks, (coupling_source, coupling_target, operator_index))[0]
    return raw_blocks * sector_mask.astype(jnp.float32)
```

```python
import jax
import jax.numpy as jnp
from jax import lax
from jax.experimental import pallas as pl
from jax.experimental.pallas import tpu as pltpu
from jax.sharding import Mesh, PartitionSpec as P

AXES = ("x_hi", "y", "x_lo", "z", "core")
SIZES = (2, 4, 2, 4, 2)
TERM = ("x_hi", "y")
SECTOR = ("x_lo", "z", "core")
LEVELS = 4
GRAIN = 128
STRIPE = 64
MIB = 1024 * 1024


def couplings_kernel(
    own_source, own_target, own_chosen, mate_meta, dims,
    own_left, mate_left, own_right, mate_right, wave,
    out_ref,
    left, right, waves, sums, sems,
):
    core = lax.axis_index("core")
    own_count = own_source.shape[0]
    ops = own_left.shape[0]
    sectors = wave.shape[0]
    copies = [
        pltpu.make_async_copy(own_left.at[:, :, core], left.at[pl.ds(0, ops)], sems.at[0]),
        pltpu.make_async_copy(mate_left, left.at[pl.ds(ops, ops)], sems.at[1]),
        pltpu.make_async_copy(own_right, right.at[pl.ds(0, ops)], sems.at[2]),
        pltpu.make_async_copy(mate_right, right.at[pl.ds(ops, ops)], sems.at[3]),
        pltpu.make_async_copy(wave, waves, sems.at[4]),
    ]
    for copy in copies:
        copy.start()
    sums[...] = jnp.zeros_like(sums)
    for copy in copies:
        copy.wait()

    def one(i, carry):
        is_own = i < own_count
        j = jnp.where(is_own, i, i - own_count)
        source = jnp.where(is_own, own_source[j], mate_meta[0, j])
        target = jnp.where(is_own, own_target[j], mate_meta[1, j])
        chosen = jnp.where(is_own, own_chosen[j], mate_meta[2, j] + ops)
        source_level = dims[source] // GRAIN
        target_level = dims[target] // GRAIN
        case = (source_level - 1) * LEVELS + target_level - 1
        for sl in range(1, LEVELS + 1):
            for tl in range(1, LEVELS + 1):

                @pl.when(case == (sl - 1) * LEVELS + tl - 1)
                def _(sl=sl, tl=tl):
                    inner, rows, cols = sl * GRAIN, tl * STRIPE, tl * GRAIN
                    block = left[chosen, :tl, :, :inner].reshape(rows, inner)
                    halfway = jnp.dot(
                        block, waves[source, :inner, :inner], preferred_element_type=jnp.float32
                    ).astype(jnp.bfloat16)
                    sums[target, :rows, :cols] += jnp.dot(
                        halfway, right[chosen, :inner, :cols], preferred_element_type=jnp.float32
                    )

        return carry

    lax.fori_loop(0, 2 * own_count, one, 0)
    parts = out_ref.shape[0]
    rows = out_ref.shape[2]
    for part in range(parts):
        out_ref[part] = sums[:, part * rows:(part + 1) * rows, :].astype(jnp.bfloat16)


def body(
    wavefunction,
    left_ops,
    right_ops,
    sector_dims,
    coupling_source,
    coupling_target,
    coupling_operator,
):
    ops, width, _ = left_ops.shape
    swap = [(0, 1), (1, 0)]
    core = lax.axis_index("core")
    striped = left_ops.reshape(ops, width // GRAIN, 2, STRIPE, width)
    other_half = lax.dynamic_index_in_dim(striped, 1 - core, 2, keepdims=False)
    meta = jnp.stack([coupling_source, coupling_target, coupling_operator])
    mate_left = lax.ppermute(other_half, "core", swap)
    mate_right = lax.ppermute(right_ops, "core", swap)
    mate_meta = lax.ppermute(meta, "core", swap)
    wave = lax.all_gather(wavefunction, SECTOR, axis=0, tiled=True)
    sectors = wave.shape[0]
    members = 8
    smem = pl.BlockSpec(memory_space=pltpu.SMEM)
    anywhere = pl.BlockSpec(memory_space=pl.ANY)
    partial = pl.pallas_call(
        couplings_kernel,
        out_shape=jax.ShapeDtypeStruct((members, sectors, width // 2 // members, width), jnp.bfloat16),
        in_specs=[smem] * 5 + [anywhere] * 5,
        out_specs=pl.BlockSpec(memory_space=pltpu.VMEM),
        scratch_shapes=[
            pltpu.VMEM((2 * ops, width // GRAIN, STRIPE, width), jnp.bfloat16),
            pltpu.VMEM((2 * ops, width, width), jnp.bfloat16),
            pltpu.VMEM((sectors, width, width), jnp.bfloat16),
            pltpu.VMEM((sectors, width // 2, width), jnp.float32),
            pltpu.SemaphoreType.DMA((5,)),
        ],
        compiler_params=pltpu.CompilerParams(vmem_limit_bytes=48 * MIB),
        name="couplings",
    )(
        coupling_source, coupling_target, coupling_operator, mate_meta, sector_dims,
        striped, mate_left, right_ops, mate_right, wave,
    )
    rows = partial.shape[2]
    sent = partial.reshape(members * sectors, rows, width)
    got = lax.all_to_all(sent, AXES, 0, 0, tiled=True)
    own = jnp.sum(got.reshape(-1, 2, rows, width).astype(jnp.float32), axis=0)
    own = own.astype(jnp.bfloat16)
    spread = jnp.broadcast_to(own[None], (members, 2, rows, width))
    whole = lax.all_to_all(spread, TERM, 0, 0, tiled=True)
    whole = whole.reshape(width // GRAIN, 2, 2, rows, width).transpose(0, 2, 1, 3, 4)
    return whole.reshape(1, width, width).astype(jnp.float32)


def solution(mesh):
    fine = Mesh(mesh.devices.reshape(SIZES), AXES)
    everyone = P(AXES)
    placed = (
        P(SECTOR, None, None),
        P(AXES, None, None),
        P(AXES, None, None),
        P(),
        everyone,
        everyone,
        everyone,
    )
    return jax.shard_map(
        body, mesh=fine, in_specs=placed, out_specs=P(SECTOR, None, None), check_vma=False
    )
```

```python
import jax
import jax.numpy as jnp
from jax import lax
from jax.experimental import pallas as pl
from jax.experimental.pallas import tpu as pltpu
from jax.sharding import Mesh, PartitionSpec as P

AXES = ("x_hi", "y", "x_lo", "z", "core")
SIZES = (2, 4, 2, 4, 2)
TERM = ("x_hi", "y")
SECTOR = ("x_lo", "z", "core")
LEVELS = 4
GRAIN = 128
STRIPE = 64
MIB = 1024 * 1024


def couplings_kernel(
    own_source, own_target, own_chosen, mate_meta, dims,
    own_left, mate_left, own_right, mate_right, wave,
    out,
    left, right, waves, halves, sums, rounded, op_sems, wave_sems, out_sems,
):
    core = lax.axis_index("core")
    own_count = own_source.shape[0]
    ops = own_left.shape[0]
    sectors = wave.shape[0]
    parts, _, rows, width = out.shape
    op_copies = [
        pltpu.make_async_copy(own_left.at[:, :, core], left.at[pl.ds(0, ops)], op_sems.at[0]),
        pltpu.make_async_copy(mate_left, left.at[pl.ds(ops, ops)], op_sems.at[1]),
        pltpu.make_async_copy(own_right, right.at[pl.ds(0, ops)], op_sems.at[2]),
        pltpu.make_async_copy(mate_right, right.at[pl.ds(ops, ops)], op_sems.at[3]),
    ]

    def wave_copy(s):
        return pltpu.make_async_copy(wave.at[s], waves.at[s], wave_sems.at[s])

    op_copies[0].start()
    op_copies[1].start()
    for s in range(sectors):
        wave_copy(s).start()
    op_copies[2].start()
    op_copies[3].start()
    sums[...] = jnp.zeros_like(sums)
    op_copies[0].wait()
    op_copies[1].wait()

    def first_half(s, carry):
        wave_copy(s).wait()
        level = dims[s] // GRAIN
        for sl in range(1, LEVELS + 1):

            @pl.when(level == sl)
            def _(sl=sl):
                inner = sl * GRAIN
                stacked = left[:, :, :, :inner].reshape(2 * ops * width // 2, inner)
                product = jnp.dot(
                    stacked, waves[s, :inner, :inner], preferred_element_type=jnp.float32
                ).astype(jnp.bfloat16)
                halves[s, :, :, :inner] = product.reshape(2 * ops, width // 2, inner)

        return carry

    lax.fori_loop(0, sectors, first_half, 0)
    op_copies[2].wait()
    op_copies[3].wait()

    def second_half(i, carry):
        is_own = i < own_count
        j = jnp.where(is_own, i, i - own_count)
        source = jnp.where(is_own, own_source[j], mate_meta[0, j])
        target = jnp.where(is_own, own_target[j], mate_meta[1, j])
        chosen = jnp.where(is_own, own_chosen[j], mate_meta[2, j] + ops)
        source_level = dims[source] // GRAIN
        target_level = dims[target] // GRAIN
        for sl in range(1, LEVELS + 1):

            @pl.when(source_level == sl)
            def _(sl=sl):
                for tl in range(1, LEVELS + 1):

                    @pl.when(target_level == tl)
                    def _(tl=tl):
                        inner, stripe, cols = sl * GRAIN, tl * STRIPE, tl * GRAIN
                        sums[target, :stripe, :cols] += jnp.dot(
                            halves[source, chosen, :stripe, :inner],
                            right[chosen, :inner, :cols],
                            preferred_element_type=jnp.float32,
                        )

        return carry

    lax.fori_loop(0, 2 * own_count, second_half, 0)
    out_copies = []
    for part in range(parts):
        rounded[part] = sums[:, part * rows:(part + 1) * rows, :].astype(jnp.bfloat16)
        copy = pltpu.make_async_copy(rounded.at[part], out.at[part], out_sems.at[part])
        copy.start()
        out_copies.append(copy)
    for copy in out_copies:
        copy.wait()


def body(
    wavefunction,
    left_ops,
    right_ops,
    sector_dims,
    coupling_source,
    coupling_target,
    coupling_operator,
):
    ops, width, _ = left_ops.shape
    swap = [(0, 1), (1, 0)]
    core = lax.axis_index("core")
    striped = left_ops.reshape(ops, width // GRAIN, 2, STRIPE, width)
    other_half = lax.dynamic_index_in_dim(striped, 1 - core, 2, keepdims=False)
    meta = jnp.stack([coupling_source, coupling_target, coupling_operator])
    mate_left = lax.ppermute(other_half, "core", swap)
    mate_right = lax.ppermute(right_ops, "core", swap)
    mate_meta = lax.ppermute(meta, "core", swap)
    wave = lax.all_gather(wavefunction, SECTOR, axis=0, tiled=True)
    sectors = wave.shape[0]
    members = 8
    smem = pl.BlockSpec(memory_space=pltpu.SMEM)
    anywhere = pl.BlockSpec(memory_space=pltpu.HBM)
    partial = pl.pallas_call(
        couplings_kernel,
        out_shape=jax.ShapeDtypeStruct((members, sectors, width // 2 // members, width), jnp.bfloat16),
        in_specs=[smem] * 5 + [anywhere] * 5,
        out_specs=anywhere,
        scratch_shapes=[
            pltpu.VMEM((2 * ops, width // GRAIN, STRIPE, width), jnp.bfloat16),
            pltpu.VMEM((2 * ops, width, width), jnp.bfloat16),
            pltpu.VMEM((sectors, width, width), jnp.bfloat16),
            pltpu.VMEM((sectors, 2 * ops, width // 2, width), jnp.bfloat16),
            pltpu.VMEM((sectors, width // 2, width), jnp.float32),
            pltpu.VMEM((members, sectors, width // 2 // members, width), jnp.bfloat16),
            pltpu.SemaphoreType.DMA((4,)),
            pltpu.SemaphoreType.DMA((sectors,)),
            pltpu.SemaphoreType.DMA((members,)),
        ],
        compiler_params=pltpu.CompilerParams(vmem_limit_bytes=56 * MIB),
        name="couplings",
    )(
        coupling_source, coupling_target, coupling_operator, mate_meta, sector_dims,
        striped, mate_left, right_ops, mate_right, wave,
    )
    rows = partial.shape[2]
    sent = partial.reshape(members * sectors, rows, width)
    got = lax.all_to_all(sent, AXES, 0, 0, tiled=True)
    own = jnp.sum(got.reshape(-1, 2, rows, width).astype(jnp.float32), axis=0)
    own = own.astype(jnp.bfloat16)
    spread = jnp.broadcast_to(own[None], (members, 2, rows, width))
    whole = lax.all_to_all(spread, TERM, 0, 0, tiled=True)
    whole = whole.reshape(width // GRAIN, 2, 2, rows, width).transpose(0, 2, 1, 3, 4)
    return whole.reshape(1, width, width).astype(jnp.float32)


def solution(mesh):
    fine = Mesh(mesh.devices.reshape(SIZES), AXES)
    everyone = P(AXES)
    placed = (
        P(SECTOR, None, None),
        P(AXES, None, None),
        P(AXES, None, None),
        P(),
        everyone,
        everyone,
        everyone,
    )
    return jax.shard_map(
        body, mesh=fine, in_specs=placed, out_specs=P(SECTOR, None, None), check_vma=False
    )
```

```python
import functools

import jax
import jax.numpy as jnp
from jax import lax
from jax.experimental import pallas as pl
from jax.experimental.pallas import tpu as pltpu
from jax.sharding import Mesh, PartitionSpec as P

AXES = ("x_hi", "y", "x_lo", "z", "core")
SIZES = (2, 4, 2, 4, 2)
SECTOR = ("x_lo", "z", "core")
FIRST = ("x_hi", "y", "x_lo")
LAST = ("x_hi", "y", "core")
MEMBERS = 8
GROUPS = 2
LEVELS = 4
GRAIN = 128
STRIPE = 64
SLICE = STRIPE // MEMBERS
PAIR_SIZES = (24, 28, 32, 36, 40, 44, 48, 56, 64)
UNROLL = 8
CHUNKS = 4
MIB = 1024 * 1024


def list_units(dims, groups):
    sectors = dims.shape[0]
    level = dims // GRAIN
    block = jnp.arange(LEVELS, dtype=jnp.int32)
    inside = (block[None, :, None] < level[:, None, None]) & (block[None, None, :] < level[:, None, None])
    inside = inside.reshape(groups, -1)
    slots = inside.shape[1]
    slot = jnp.arange(slots, dtype=jnp.int32)
    before = (slot[:, None] <= slot[None, :]).astype(jnp.int32)
    place = jnp.sum(inside[:, :, None] * before[None], axis=1) - 1
    here = inside[:, :, None] & (place[:, :, None] == slot[None, None, :])
    table = jnp.sum(jnp.where(here, slot[None, :, None], 0), axis=1)
    return table, jnp.sum(inside.astype(jnp.int32), axis=1)


def couplings_kernel(
    own_source, own_target, own_chosen, mate_meta, dims, table,
    own_left, mate_left, own_right, mate_right, wave,
    out,
    left, right, waves, halves, sums, packed, op_sems, wave_sems, out_sems,
):
    core = lax.axis_index("core")
    own_count = own_source.shape[0]
    ops = own_left.shape[0]
    sectors, width, _ = wave.shape
    half = width // 2
    pairs = out.shape[2]
    op_copies = [
        pltpu.make_async_copy(own_left.at[:, :, core], left.at[pl.ds(0, ops)], op_sems.at[0]),
        pltpu.make_async_copy(mate_left, left.at[pl.ds(ops, ops)], op_sems.at[1]),
        pltpu.make_async_copy(own_right, right.at[pl.ds(0, ops)], op_sems.at[2]),
        pltpu.make_async_copy(mate_right, right.at[pl.ds(ops, ops)], op_sems.at[3]),
    ]

    def wave_copy(s):
        return pltpu.make_async_copy(wave.at[s], waves.at[s], wave_sems.at[s])

    op_copies[0].start()
    op_copies[1].start()
    for s in range(sectors):
        wave_copy(s).start()
    op_copies[2].start()
    op_copies[3].start()
    in_group = sectors // GROUPS
    op_copies[0].wait()
    op_copies[1].wait()

    def first_half(s, carry):
        wave_copy(s).wait()
        level = dims[s] // GRAIN
        for sl in range(1, LEVELS + 1):

            @pl.when(level == sl)
            def _(sl=sl):
                inner = sl * GRAIN
                blank = jnp.zeros((LEVELS, half, GRAIN), jnp.float32)
                sums[pl.ds(s * LEVELS, LEVELS)] = blank
                stacked = left[:, :, :, :inner].reshape(2 * ops * half, inner)
                product = jnp.dot(
                    stacked, waves[s, :inner, :inner], preferred_element_type=jnp.float32
                ).astype(jnp.bfloat16)
                halves[s, :, :, :inner] = product.reshape(2 * ops, half, inner)
                if inner < width:
                    halves[s, :, :, inner:] = jnp.zeros((2 * ops, half, width - inner), jnp.bfloat16)

        return carry

    lax.fori_loop(0, sectors, first_half, 0)
    op_copies[2].wait()
    op_copies[3].wait()

    def second_half(source, target, chosen):
        product = jnp.dot(
            halves[source, chosen], right[chosen], preferred_element_type=jnp.float32
        )
        for c in range(LEVELS):
            sums[target * LEVELS + c] += product[:, c * GRAIN:(c + 1) * GRAIN]

    def own_step(i, carry):
        for u in range(UNROLL):
            j = i * UNROLL + u
            second_half(own_source[j], own_target[j], own_chosen[j])
        return carry

    def mate_step(i, carry):
        for u in range(UNROLL):
            j = i * UNROLL + u
            second_half(mate_meta[0, j], mate_meta[1, j], mate_meta[2, j] + ops)
        return carry

    lax.fori_loop(0, own_count // UNROLL, own_step, 0)
    lax.fori_loop(0, own_count // UNROLL, mate_step, 0)

    copies = []
    for group in range(GROUPS):
        offset = group * in_group * LEVELS

        def pack(p, carry, group=group, offset=offset):
            a, b = table[group, 2 * p], table[group, 2 * p + 1]
            a_block, a_row = offset + lax.div(a, LEVELS), lax.rem(a, LEVELS) * STRIPE
            b_block, b_row = offset + lax.div(b, LEVELS), lax.rem(b, LEVELS) * STRIPE
            for k in range(MEMBERS):
                top = sums[a_block, pl.ds(pl.multiple_of(a_row + k * SLICE, SLICE), SLICE), :]
                low = sums[b_block, pl.ds(pl.multiple_of(b_row + k * SLICE, SLICE), SLICE), :]
                both = jnp.concatenate([top, low], axis=0).astype(jnp.bfloat16)
                packed[group, k, p] = both
            return carry

        lax.fori_loop(0, pairs, pack, 0)
        copy = pltpu.make_async_copy(packed.at[group], out.at[:, group], out_sems.at[group])
        copy.start()
        copies.append(copy)
    for copy in copies:
        copy.wait()


def unpack_kernel(table, counts, got, out, here, sems):
    group = lax.axis_index("x_lo")
    sources, pairs = got.shape[0], got.shape[1]
    step = pairs // CHUNKS
    copies = []
    for chunk in range(CHUNKS):
        part = pl.ds(chunk * step, step)
        copy = pltpu.make_async_copy(got.at[:, part], here.at[:, part], sems.at[chunk])
        copy.start()
        copies.append(copy)
    out[...] = jnp.zeros_like(out)
    used = counts[group]

    def one(n):
        code = table[group, n]
        s = lax.div(code, LEVELS * LEVELS)
        column = lax.rem(lax.div(code, LEVELS), LEVELS)
        row = lax.rem(code, LEVELS)
        return s, row * LEVELS + column

    def both(p, carry):
        total = here[0, p].astype(jnp.float32)
        for k in range(1, sources):
            total += here[k, p].astype(jnp.float32)

        @pl.when(2 * p < used)
        def _():
            s, u = one(2 * p)
            out[s, u] = total[:SLICE]

        @pl.when(2 * p + 1 < used)
        def _():
            s, u = one(2 * p + 1)
            out[s, u] = total[SLICE:]

        return carry

    for chunk in range(CHUNKS):
        copies[chunk].wait()
        lax.fori_loop(chunk * step, (chunk + 1) * step, both, 0)


def body(
    wavefunction,
    left_ops,
    right_ops,
    sector_dims,
    coupling_source,
    coupling_target,
    coupling_operator,
):
    ops, width, _ = left_ops.shape
    swap = [(0, 1), (1, 0)]
    core = lax.axis_index("core")
    striped = left_ops.reshape(ops, width // GRAIN, 2, STRIPE, width)
    other_half = lax.dynamic_index_in_dim(striped, 1 - core, 2, keepdims=False)
    meta = jnp.stack([coupling_source, coupling_target, coupling_operator])
    mate_left = lax.ppermute(other_half, "core", swap)
    mate_right = lax.ppermute(right_ops, "core", swap)
    mate_meta = lax.ppermute(meta, "core", swap)
    wave = lax.all_gather(wavefunction, SECTOR, axis=0, tiled=True)
    sectors = wave.shape[0]
    in_group = sectors // GROUPS
    smem = pl.BlockSpec(memory_space=pltpu.SMEM)
    hbm = pl.BlockSpec(memory_space=pltpu.HBM)
    vmem = pl.BlockSpec(memory_space=pltpu.VMEM)

    def exchange(pairs, operands, counts):
        packed = (MEMBERS, GROUPS, pairs, 2 * SLICE, GRAIN)
        partial = pl.pallas_call(
            couplings_kernel,
            out_shape=jax.ShapeDtypeStruct(packed, jnp.bfloat16),
            in_specs=[smem] * 6 + [hbm] * 5,
            out_specs=hbm,
            scratch_shapes=[
                pltpu.VMEM((2 * ops, width // GRAIN, STRIPE, width), jnp.bfloat16),
                pltpu.VMEM((2 * ops, width, width), jnp.bfloat16),
                pltpu.VMEM((sectors, width, width), jnp.bfloat16),
                pltpu.VMEM((sectors, 2 * ops, width // 2, width), jnp.bfloat16),
                pltpu.VMEM((sectors * LEVELS, width // 2, GRAIN), jnp.float32),
                pltpu.VMEM((GROUPS, MEMBERS) + packed[2:], jnp.bfloat16),
                pltpu.SemaphoreType.DMA((4,)),
                pltpu.SemaphoreType.DMA((sectors,)),
                pltpu.SemaphoreType.DMA((GROUPS,)),
            ],
            compiler_params=pltpu.CompilerParams(vmem_limit_bytes=56 * MIB),
            name="couplings",
        )(*operands)
        partial = partial.reshape((MEMBERS * GROUPS,) + packed[2:])
        got = lax.all_to_all(partial, FIRST, 0, 0, tiled=True)
        return pl.pallas_call(
            unpack_kernel,
            out_shape=jax.ShapeDtypeStruct((in_group, LEVELS * LEVELS, SLICE, GRAIN), jnp.float32),
            in_specs=[smem, smem, hbm],
            out_specs=vmem,
            scratch_shapes=[
                pltpu.VMEM(got.shape, jnp.bfloat16),
                pltpu.SemaphoreType.DMA((CHUNKS,)),
            ],
            compiler_params=pltpu.CompilerParams(vmem_limit_bytes=32 * MIB),
            name="unpack",
        )(operands[5], counts, got)

    table, counts = list_units(sector_dims, GROUPS)
    units = jnp.max(counts)
    which = jnp.sum((units > 2 * jnp.array(PAIR_SIZES[:-1], jnp.int32)).astype(jnp.int32))
    operands = (
        coupling_source, coupling_target, coupling_operator, mate_meta, sector_dims, table,
        striped, mate_left, right_ops, mate_right, wave,
    )
    share = lax.switch(which, [functools.partial(exchange, pairs) for pairs in PAIR_SIZES], operands, counts)
    share = lax.all_to_all(share, "z", 0, 0, tiled=True)
    share = jnp.sum(share.reshape(-1, 2, LEVELS * LEVELS // 2, 2 * SLICE, GRAIN), axis=0)
    share = share.astype(jnp.bfloat16)
    spread = jnp.broadcast_to(share[None], (MEMBERS,) + share.shape)
    spread = spread.reshape((2 * MEMBERS,) + share.shape[1:])
    whole = lax.all_to_all(spread, LAST, 0, 0, tiled=True)
    whole = whole.reshape(MEMBERS, 2, LEVELS, 2, 2, SLICE, GRAIN).transpose(2, 1, 0, 5, 3, 4, 6)
    return whole.reshape(1, width, width).astype(jnp.float32)


def solution(mesh):
    fine = Mesh(mesh.devices.reshape(SIZES), AXES)
    everyone = P(AXES)
    placed = (
        P(SECTOR, None, None),
        P(AXES, None, None),
        P(AXES, None, None),
        P(),
        everyone,
        everyone,
        everyone,
    )
    return jax.shard_map(
        body, mesh=fine, in_specs=placed, out_specs=P(SECTOR, None, None), check_vma=False
    )
```

```python
import jax
import jax.numpy as jnp
from jax import lax
from jax.experimental import pallas as pl
from jax.experimental.pallas import tpu as pltpu
from jax.sharding import Mesh, PartitionSpec as P

AXES = ("x_hi", "y", "x_lo", "z", "core")
SIZES = (2, 4, 2, 4, 2)
SECTOR = ("x_lo", "z", "core")
SHARERS = ("y", "core")
REDUCE = ("x_hi", "x_lo", "z")
SPREAD = ("x_hi", "y", "core")
RING = 4
GROUP = 8
LEVELS = 4
GRAIN = 128
SLICE = GRAIN // GROUP
STACK = 4
UNROLL = 2
MIB = 1024 * 1024


def plan_couplings(source, target, chosen, operators, sectors):
    count = source.shape[0]
    stacks = -(-(count + operators * (STACK - 1)) // STACK)
    stacks = -(-stacks // UNROLL) * UNROLL
    is_op = chosen[:, None] == jnp.arange(operators, dtype=jnp.int32)[None, :]
    number = jnp.sum(is_op.astype(jnp.int32), axis=0)
    taken = (number + STACK - 1) // STACK
    op = jnp.arange(operators, dtype=jnp.int32)
    end = jnp.sum(jnp.where(op[:, None] <= op[None, :], taken[:, None], 0), axis=0)
    start = end - taken
    spot = jnp.arange(count, dtype=jnp.int32)
    earlier = (chosen[:, None] == chosen[None, :]) & (spot[:, None] < spot[None, :])
    rank = jnp.sum(earlier.astype(jnp.int32), axis=0)
    place = rank + STACK * jnp.sum(jnp.where(is_op, start[None, :], 0), axis=1)
    here = place[:, None] == jnp.arange(stacks * STACK, dtype=jnp.int32)[None, :]
    code = source * (2 * sectors) + target - sectors
    table = sectors + jnp.sum(jnp.where(here, code[:, None], 0), axis=0)
    stack = jnp.arange(stacks, dtype=jnp.int32)
    stack_op = jnp.sum((end[:, None] <= stack[None, :]).astype(jnp.int32), axis=0)
    return table, jnp.minimum(stack_op, operators - 1), jnp.max(end)[None]


def couplings_kernel(
    table, stack_op, stack_count, dims,
    left_rows, own, own_down, own_up, own_far_a, own_far_b,
    mate, mate_down, mate_up, mate_far_a, mate_far_b, wave,
    out,
    left, right, waves, halves, sums, op_sems, wave_sems,
):
    y, core = lax.axis_index("y"), lax.axis_index("core")
    sectors, width, _ = wave.shape
    rows = sums.shape[1]
    ops = own.shape[0]

    def wave_copy(s):
        return pltpu.make_async_copy(wave.at[s], waves.at[s], wave_sems.at[s])

    left_copy = pltpu.make_async_copy(left_rows, left, op_sems.at[0])
    left_copy.start()
    for s in range(sectors):
        wave_copy(s).start()
    right_copies = []
    for c, parts in (
        (core, (own, own_down, own_up, own_far_a, own_far_b)),
        (1 - core, (mate, mate_down, mate_up, mate_far_a, mate_far_b)),
    ):
        for part, (shift, first) in zip(parts, ((0, 0), (RING - 1, 0), (1, 0), (2, 0), (2, 1))):
            slot = (lax.rem(y + shift, RING) * 2 + c) * ops + first
            copy = pltpu.make_async_copy(
                part, right.at[pl.ds(slot, part.shape[0])], op_sems.at[1 + len(right_copies)]
            )
            copy.start()
            right_copies.append(copy)
    sums[...] = jnp.zeros_like(sums)
    left_copy.wait()

    def first_half(s, carry):
        wave_copy(s).wait()
        level = dims[s] // GRAIN
        for sl in range(1, LEVELS + 1):

            @pl.when(level == sl)
            def _(sl=sl):
                inner = sl * GRAIN
                halves[s, :, :inner] = jnp.dot(
                    left[:, :inner], waves[s, :inner, :inner], preferred_element_type=jnp.float32
                ).astype(jnp.bfloat16)
                if inner < width:
                    halves[s, :, inner:] = jnp.zeros((left.shape[0], width - inner), jnp.bfloat16)

        return carry

    lax.fori_loop(0, sectors, first_half, 0)
    for copy in right_copies:
        copy.wait()

    def second_half(i, carry):
        for u in range(UNROLL):
            j = i * UNROLL + u
            op = stack_op[j]
            first = pl.multiple_of(op * rows, rows)
            codes = [table[j * STACK + k] for k in range(STACK)]
            sources = [lax.div(code, 2 * sectors) for code in codes]
            stacked = jnp.concatenate([halves[s, pl.ds(first, rows), :] for s in sources], axis=0)
            product = jnp.dot(stacked, right[op], preferred_element_type=jnp.float32)
            for k in range(STACK):
                target = lax.rem(codes[k], 2 * sectors)
                sums[target] += product[k * rows:(k + 1) * rows]
        return carry

    lax.fori_loop(0, lax.div(stack_count[0] + UNROLL - 1, UNROLL), second_half, 0)
    parts = out.shape[0]
    size = rows // parts
    for part in range(parts):
        out[part] = sums[:sectors, part * size:(part + 1) * size, :].astype(jnp.bfloat16)


def share_operators(left_ops, right_ops, meta):
    ops, width, _ = left_ops.shape
    down = [(i, (i + 1) % RING) for i in range(RING)]
    up = [(i, (i - 1) % RING) for i in range(RING)]
    swap = [(0, 1), (1, 0)]
    from_down = lax.ppermute(right_ops, "y", down)
    from_up = lax.ppermute(right_ops, "y", up)
    far_a = lax.ppermute(from_down[:1], "y", down)
    far_b = lax.ppermute(from_up[1:], "y", up)
    own = (right_ops, from_down, from_up, far_a, far_b)
    mate = tuple(lax.ppermute(part, "core", swap) for part in own)
    metas = lax.all_to_all(jnp.broadcast_to(meta[None], (GROUP,) + meta.shape), SHARERS, 0, 0, tiled=True)
    rows = left_ops.reshape(ops, width // GRAIN, GROUP, SLICE, width).transpose(2, 0, 1, 3, 4)
    left_rows = lax.all_to_all(rows, SHARERS, 0, 0, tiled=True)
    return left_rows.reshape(ops * width, width), own + mate, metas


def body(
    wavefunction,
    left_ops,
    right_ops,
    sector_dims,
    coupling_source,
    coupling_target,
    coupling_operator,
):
    ops, width, _ = left_ops.shape
    wave = lax.all_gather(wavefunction, SECTOR, axis=0, tiled=True)
    sectors = wave.shape[0]
    meta = jnp.stack([coupling_source, coupling_target, coupling_operator])
    left_rows, rights, metas = share_operators(left_ops, right_ops, meta)
    first_op = ops * jnp.arange(GROUP, dtype=jnp.int32)[:, None]
    table, stack_op, stack_count = plan_couplings(
        metas[:, 0].reshape(-1), metas[:, 1].reshape(-1), (metas[:, 2] + first_op).reshape(-1),
        ops * GROUP, sectors,
    )
    smem = pl.BlockSpec(memory_space=pltpu.SMEM)
    hbm = pl.BlockSpec(memory_space=pltpu.HBM)
    vmem = pl.BlockSpec(memory_space=pltpu.VMEM)
    rows = width // GROUP
    partial = pl.pallas_call(
        couplings_kernel,
        out_shape=jax.ShapeDtypeStruct((2, sectors, rows // 2, width), jnp.bfloat16),
        in_specs=[smem] * 4 + [hbm] * 12,
        out_specs=vmem,
        scratch_shapes=[
            pltpu.VMEM((ops * width, width), jnp.bfloat16),
            pltpu.VMEM((ops * GROUP, width, width), jnp.bfloat16),
            pltpu.VMEM((sectors, width, width), jnp.bfloat16),
            pltpu.VMEM((sectors, ops * width, width), jnp.bfloat16),
            pltpu.VMEM((sectors + 1, rows, width), jnp.float32),
            pltpu.SemaphoreType.DMA((11,)),
            pltpu.SemaphoreType.DMA((sectors,)),
        ],
        compiler_params=pltpu.CompilerParams(vmem_limit_bytes=56 * MIB),
        name="couplings",
    )(table, stack_op, stack_count, sector_dims, left_rows, *rights, wave)
    got = lax.all_to_all(partial.reshape(sectors, 2, rows // 2, width), REDUCE, 0, 0, tiled=True)
    share = jnp.sum(got.astype(jnp.float32), axis=0)
    x_hi, y, core = (lax.axis_index(name) for name in SPREAD)
    place = jnp.arange(rows // 2, dtype=jnp.int32)
    row = (x_hi * 2 + place // SLICE) * GRAIN + (y * 2 + core) * SLICE + place % SLICE
    column = jnp.arange(width, dtype=jnp.int32)
    own_pair = lax.axis_index("x_lo") * RING + lax.axis_index("z")
    limit = lax.dynamic_slice_in_dim(sector_dims, 2 * own_pair, 2)[:, None, None]
    kept = (row[None, :, None] < limit) & (column[None, None, :] < limit)
    share = jnp.where(kept, share, 0.0).astype(jnp.bfloat16)
    spread = jnp.broadcast_to(share[None], (GROUP,) + share.shape).reshape((2 * GROUP,) + share.shape[1:])
    whole = lax.all_to_all(spread, SPREAD, 0, 0, tiled=True)
    whole = whole.reshape(2, GROUP, 2, SLICE, width).transpose(0, 2, 1, 3, 4)
    return whole.reshape(1, width, width).astype(jnp.float32)


def solution(mesh):
    fine = Mesh(mesh.devices.reshape(SIZES), AXES)
    everyone = P(AXES)
    placed = (
        P(SECTOR, None, None),
        P(AXES, None, None),
        P(AXES, None, None),
        P(),
        everyone,
        everyone,
        everyone,
    )
    return jax.shard_map(
        body, mesh=fine, in_specs=placed, out_specs=P(SECTOR, None, None), check_vma=False
    )
```

```python
import jax
import jax.numpy as jnp
from jax import lax
from jax.experimental import pallas as pl
from jax.experimental.pallas import tpu as pltpu
from jax.sharding import Mesh, PartitionSpec as P

AXES = ("x_hi", "y_hi", "y_lo", "x_lo", "z", "core")
SIZES = (2, 2, 2, 2, 4, 2)
SECTOR = ("x_lo", "z", "core")
SHARERS = ("y_lo", "core")
REDUCE = ("x_hi", "y_hi", "x_lo", "z")
SPREAD = ("x_hi", "y_hi", "y_lo", "core")
RING = 4
GROUP = 4
LEVELS = 4
GRAIN = 128
SLICE = GRAIN // GROUP
STACK = 4
UNROLL = 2
MIB = 1024 * 1024
SWAP = [(0, 1), (1, 0)]
UP = [(i, (i + 1) % RING) for i in range(RING)]
DOWN = [(i, (i - 1) % RING) for i in range(RING)]
SHIFTS = (0, RING - 1, 1, 2)


def plan_couplings(source, target, chosen, operators, sectors):
    count = source.shape[0]
    stacks = -(-(count + operators * (STACK - 1)) // STACK)
    stacks = -(-stacks // UNROLL) * UNROLL
    is_op = chosen[:, None] == jnp.arange(operators, dtype=jnp.int32)[None, :]
    number = jnp.sum(is_op.astype(jnp.int32), axis=0)
    taken = (number + STACK - 1) // STACK
    op = jnp.arange(operators, dtype=jnp.int32)
    end = jnp.sum(jnp.where(op[:, None] <= op[None, :], taken[:, None], 0), axis=0)
    start = end - taken
    spot = jnp.arange(count, dtype=jnp.int32)
    earlier = (chosen[:, None] == chosen[None, :]) & (spot[:, None] < spot[None, :])
    rank = jnp.sum(earlier.astype(jnp.int32), axis=0)
    place = rank + STACK * jnp.sum(jnp.where(is_op, start[None, :], 0), axis=1)
    here = place[:, None] == jnp.arange(stacks * STACK, dtype=jnp.int32)[None, :]
    code = source * (2 * sectors) + target - sectors
    table = sectors + jnp.sum(jnp.where(here, code[:, None], 0), axis=0)
    stack = jnp.arange(stacks, dtype=jnp.int32)
    stack_op = jnp.sum((end[:, None] <= stack[None, :]).astype(jnp.int32), axis=0)
    return table, jnp.minimum(stack_op, operators - 1), jnp.max(end)[None]


def couplings_kernel(table, stack_op, stack_count, dims, *refs):
    own_waves, mate_waves = refs[:11], refs[11:22]
    own_right, own_left, mate_right, mate_left, far_right, far_left, far_mate_right, far_mate_left = refs[22:30]
    out, left, right, waves, halves, sums, op_sems, wave_sems = refs[30:]
    y, x, z, core = (lax.axis_index(name) for name in ("y_lo", "x_lo", "z", "core"))
    sectors, width, _ = waves.shape
    rows = sums.shape[1]
    ops = own_right.shape[0]
    half = width // 2
    left_copies, right_copies = [], []
    for n, (pair, c, left_rows, right_ops) in enumerate((
        (y, core, own_left, own_right),
        (y, 1 - core, mate_left, mate_right),
        (1 - y, core, far_left, far_right),
        (1 - y, 1 - core, far_mate_left, far_mate_right),
    )):
        first = (pair * 2 + c) * ops
        size = ops * rows
        to = left.at[pl.ds(pl.multiple_of(first * rows, size), size)]
        left_copies.append(pltpu.make_async_copy(left_rows.at[core], to, op_sems.at[2 * n]))
        right_copies.append(
            pltpu.make_async_copy(right_ops, right.at[pl.ds(first, ops)], op_sems.at[2 * n + 1])
        )
    for copy in left_copies:
        copy.start()
    whole, low, high = (pl.ds(0, width), pl.ds(0, half), pl.ds(half, half))
    places = (
        (0, whole), (1, whole), (2, whole), (3, low), (3, high),
        (4, low), (4, high), (5, whole), (6, whole), (7, low), (7, high),
    )
    for c, pieces in ((0, own_waves), (1, mate_waves)):
        for piece, (place, part) in zip(pieces, places):
            slot = c * (sectors // 2) + place
            pltpu.make_async_copy(piece, waves.at[slot, part], wave_sems.at[slot]).start()
    for copy in right_copies:
        copy.start()
    sums[...] = jnp.zeros_like(sums)
    for copy in left_copies:
        copy.wait()

    def first_half(slot, carry):
        pltpu.make_async_copy(waves.at[slot], waves.at[slot], wave_sems.at[slot]).wait()
        other_core = lax.div(slot, sectors // 2)
        other_x = lax.rem(lax.div(slot, RING), 2)
        step = lax.rem(slot, RING)
        shift = jnp.where(step == 1, RING - 1, jnp.where(step == 2, 1, jnp.where(step == 3, 2, 0)))
        x_at = lax.rem(x + other_x, 2)
        core_at = lax.rem(core + other_core, 2)
        s = (x_at * RING + lax.rem(z + shift, RING)) * 2 + core_at
        level = dims[s] // GRAIN
        for sl in range(1, LEVELS + 1):

            @pl.when(level == sl)
            def _(sl=sl):
                inner = sl * GRAIN
                halves[s, :, :inner] = jnp.dot(
                    left[:, :inner], waves[slot, :inner, :inner], preferred_element_type=jnp.float32
                ).astype(jnp.bfloat16)
                if inner < width:
                    halves[s, :, inner:] = jnp.zeros((left.shape[0], width - inner), jnp.bfloat16)

        return carry

    lax.fori_loop(0, sectors, first_half, 0)
    for copy in right_copies:
        copy.wait()

    def second_half(i, carry):
        for u in range(UNROLL):
            j = i * UNROLL + u
            op = stack_op[j]
            first = pl.multiple_of(op * rows, rows)
            codes = [table[j * STACK + k] for k in range(STACK)]
            sources = [lax.div(code, 2 * sectors) for code in codes]
            stacked = jnp.concatenate([halves[s, pl.ds(first, rows), :] for s in sources], axis=0)
            product = jnp.dot(stacked, right[op], preferred_element_type=jnp.float32)
            for k in range(STACK):
                target = lax.rem(codes[k], 2 * sectors)
                sums[target] += product[k * rows:(k + 1) * rows]
        return carry

    lax.fori_loop(0, lax.div(stack_count[0] + UNROLL - 1, UNROLL), second_half, 0)
    parts = out.shape[0]
    size = rows // parts
    for part in range(parts):
        out[part] = sums[:sectors, part * size:(part + 1) * size, :].astype(jnp.bfloat16)


def along_x(part, steps):
    return lax.ppermute(part, ("x_hi", "x_lo"), steps)


def to_mate(part):
    return lax.ppermute(part, "core", SWAP)


def share(block, left_ops, right_ops, meta):
    ops, width, _ = left_ops.shape
    half = width // 2
    rows = left_ops.reshape(ops, LEVELS, 2, 2, SLICE, width).transpose(2, 3, 0, 1, 4, 5)
    rows = rows.reshape(2, 2, ops * LEVELS * SLICE, width)
    y = lax.axis_index("y_lo")
    near_rows = lax.dynamic_index_in_dim(rows, y, 0, keepdims=False)
    sent_rows = lax.dynamic_index_in_dim(rows, 1 - y, 0, keepdims=False)
    far_right = lax.ppermute(right_ops, "y_lo", SWAP)
    far_rows = lax.ppermute(sent_rows, "y_lo", SWAP)
    before = lax.ppermute(block, "z", UP)
    after = lax.ppermute(block, "z", DOWN)
    side_low = along_x(block[:half], UP)
    side_high = along_x(block[half:], DOWN)
    across_low = lax.ppermute(before[:half], "z", UP)
    across_high = lax.ppermute(after[half:], "z", DOWN)
    side_before = along_x(before, UP)
    side_after = along_x(after, DOWN)
    corner_low = along_x(across_low, UP)
    corner_high = along_x(across_high, DOWN)
    metas = lax.all_to_all(jnp.broadcast_to(meta[None], (GROUP,) + meta.shape), SHARERS, 0, 0, tiled=True)
    early = (
        block, before, after, across_low, across_high, side_low, side_high, side_before, side_after,
    )
    own_waves = early + (corner_low, corner_high)
    held = lax.optimization_barrier(early + (right_ops, near_rows, metas))
    metas = held[-1]
    mate_early = [to_mate(part) for part in held[:-1]]
    mate_late = [to_mate(part) for part in lax.optimization_barrier((corner_low, corner_high, far_right, far_rows))]
    mate_waves = tuple(mate_early[:9] + mate_late[:2])
    operators = (right_ops, near_rows, mate_early[9], mate_early[10], far_right, far_rows, mate_late[2], mate_late[3])
    return own_waves + mate_waves + operators, metas


def body(
    wavefunction,
    left_ops,
    right_ops,
    sector_dims,
    coupling_source,
    coupling_target,
    coupling_operator,
):
    ops, width, _ = left_ops.shape
    sectors = 4 * RING
    meta = jnp.stack([coupling_source, coupling_target, coupling_operator])
    shared, metas = share(wavefunction[0], left_ops, right_ops, meta)
    first_op = ops * jnp.arange(GROUP, dtype=jnp.int32)[:, None]
    table, stack_op, stack_count = plan_couplings(
        metas[:, 0].reshape(-1), metas[:, 1].reshape(-1), (metas[:, 2] + first_op).reshape(-1),
        ops * GROUP, sectors,
    )
    smem = pl.BlockSpec(memory_space=pltpu.SMEM)
    hbm = pl.BlockSpec(memory_space=pltpu.HBM)
    vmem = pl.BlockSpec(memory_space=pltpu.VMEM)
    rows = width // GROUP
    partial = pl.pallas_call(
        couplings_kernel,
        out_shape=jax.ShapeDtypeStruct((LEVELS, sectors, SLICE, width), jnp.bfloat16),
        in_specs=[smem] * 4 + [hbm] * len(shared),
        out_specs=vmem,
        scratch_shapes=[
            pltpu.VMEM((ops * width, width), jnp.bfloat16),
            pltpu.VMEM((ops * GROUP, width, width), jnp.bfloat16),
            pltpu.VMEM((sectors, width, width), jnp.bfloat16),
            pltpu.VMEM((sectors, ops * width, width), jnp.bfloat16),
            pltpu.VMEM((sectors + 1, rows, width), jnp.float32),
            pltpu.SemaphoreType.DMA((8,)),
            pltpu.SemaphoreType.DMA((sectors,)),
        ],
        compiler_params=pltpu.CompilerParams(vmem_limit_bytes=56 * MIB),
        name="couplings",
    )(table, stack_op, stack_count, sector_dims, *shared)
    got = lax.all_to_all(partial.reshape(-1, 2, SLICE, width), REDUCE, 0, 0, tiled=True)
    total = jnp.sum(got.astype(jnp.float32), axis=0)
    x_hi, y_hi, y_lo, core = (lax.axis_index(name) for name in SPREAD)
    row = (((x_hi * 2 + y_hi) * 2 + y_lo) * 2 + core) * SLICE + jnp.arange(SLICE, dtype=jnp.int32)
    column = jnp.arange(width, dtype=jnp.int32)
    own_pair = lax.axis_index("x_lo") * RING + lax.axis_index("z")
    limit = lax.dynamic_slice_in_dim(sector_dims, 2 * own_pair, 2)[:, None, None]
    kept = (row[None, :, None] < limit) & (column[None, None, :] < limit)
    total = jnp.where(kept, total, 0.0).astype(jnp.bfloat16)
    spread = jnp.broadcast_to(total[None], (8,) + total.shape).reshape((16,) + total.shape[1:])
    whole = lax.all_to_all(spread, SPREAD, 0, 0, tiled=True)
    return whole.reshape(1, width, width).astype(jnp.float32)


def solution(mesh):
    fine = Mesh(mesh.devices.reshape(SIZES), AXES)
    everyone = P(AXES)
    placed = (
        P(SECTOR, None, None),
        P(AXES, None, None),
        P(AXES, None, None),
        P(),
        everyone,
        everyone,
        everyone,
    )
    return jax.shard_map(
        body, mesh=fine, in_specs=placed, out_specs=P(SECTOR, None, None), check_vma=False
    )
```

```python
import jax
import jax.numpy as jnp
from jax import lax
from jax.experimental import pallas as pl
from jax.experimental.pallas import tpu as pltpu
from jax.sharding import Mesh, PartitionSpec as P

AXES = ("x_hi", "y_hi", "y_lo", "x_lo", "z", "core")
SIZES = (2, 2, 2, 2, 4, 2)
SECTOR = ("x_lo", "z", "core")
REDUCE = ("x_hi", "y_hi", "x_lo", "z")
SPREAD = ("x_hi", "y_hi", "y_lo", "core")
RING = 4
GROUP = 4
LEVELS = 4
GRAIN = 128
SLICE = GRAIN // GROUP
STEP = 8
KINDS = 4
MIB = 1024 * 1024
SWAP = [(0, 1), (1, 0)]
UP = [(i, (i + 1) % RING) for i in range(RING)]
DOWN = [(i, (i - 1) % RING) for i in range(RING)]
SHIFTS = (0, RING - 1, 1, 2)


def plan_couplings(source, target, op, dims, half):
    sectors = dims.shape[0]
    count = source.shape[0]
    steps = (count + KINDS * (STEP - 1)) // STEP
    index = jnp.arange(sectors, dtype=jnp.int32)[None, :]
    wide = (dims > half).astype(jnp.int32)[None, :]
    wide_source = jnp.sum(jnp.where(source[:, None] == index, wide, 0), axis=1)
    wide_target = jnp.sum(jnp.where(target[:, None] == index, wide, 0), axis=1)
    kind = 2 * wide_source + wide_target
    kinds = jnp.arange(KINDS, dtype=jnp.int32)
    is_kind = kind[:, None] == kinds[None, :]
    taken = (jnp.sum(is_kind.astype(jnp.int32), axis=0) + STEP - 1) // STEP
    end = jnp.sum(jnp.where(kinds[:, None] <= kinds[None, :], taken[:, None], 0), axis=0)
    start = end - taken
    spot = jnp.arange(count, dtype=jnp.int32)
    earlier = (kind[:, None] == kind[None, :]) & (spot[:, None] < spot[None, :])
    rank = jnp.sum(earlier.astype(jnp.int32), axis=0)
    place = rank + STEP * jnp.sum(jnp.where(is_kind, start[None, :], 0), axis=1)
    here = place[:, None] == jnp.arange(steps * STEP, dtype=jnp.int32)[None, :]
    code = (op * sectors + source) * (2 * sectors) + target - sectors
    return sectors + jnp.sum(jnp.where(here, code[:, None], 0), axis=0), end


def couplings_kernel(table, ends, dims, *refs):
    own_waves, mate_waves = refs[:11], refs[11:22]
    own_right, own_left, mate_right, mate_left, far_right, far_left, far_mate_right, far_mate_left = refs[22:30]
    out, left, right, waves, halves, sums, rounded, op_sems, wave_sems, out_sems = refs[30:]
    y, x, z, core = (lax.axis_index(name) for name in ("y_lo", "x_lo", "z", "core"))
    sectors, width, _ = waves.shape
    rows = sums.shape[1]
    ops = own_right.shape[0]
    half = width // 2
    left_copies, right_copies = [], []
    for n, (pair, c, left_rows, right_ops) in enumerate((
        (y, core, own_left, own_right),
        (y, 1 - core, mate_left, mate_right),
        (1 - y, core, far_left, far_right),
        (1 - y, 1 - core, far_mate_left, far_mate_right),
    )):
        first = (pair * 2 + c) * ops
        size = ops * rows
        to = left.at[pl.ds(pl.multiple_of(first * rows, size), size)]
        left_copies.append(pltpu.make_async_copy(left_rows.at[core], to, op_sems.at[2 * n]))
        right_copies.append(
            pltpu.make_async_copy(right_ops, right.at[pl.ds(first, ops)], op_sems.at[2 * n + 1])
        )
    for copy in left_copies:
        copy.start()
    whole, low, high = (pl.ds(0, width), pl.ds(0, half), pl.ds(half, half))
    places = (
        (0, whole), (1, whole), (2, whole), (3, low), (3, high),
        (4, low), (4, high), (5, whole), (6, whole), (7, low), (7, high),
    )
    for c, pieces in ((0, own_waves), (1, mate_waves)):
        for piece, (place, part) in zip(pieces, places):
            slot = c * (sectors // 2) + place
            pltpu.make_async_copy(piece, waves.at[slot, part], wave_sems.at[slot]).start()
    for copy in right_copies:
        copy.start()
    sums[...] = jnp.zeros_like(sums)
    for copy in left_copies:
        copy.wait()

    def first_half(slot, carry):
        pltpu.make_async_copy(waves.at[slot], waves.at[slot], wave_sems.at[slot]).wait()
        other_core = lax.div(slot, sectors // 2)
        other_x = lax.rem(lax.div(slot, RING), 2)
        step = lax.rem(slot, RING)
        shift = jnp.where(step == 1, RING - 1, jnp.where(step == 2, 1, jnp.where(step == 3, 2, 0)))
        x_at = lax.rem(x + other_x, 2)
        core_at = lax.rem(core + other_core, 2)
        s = (x_at * RING + lax.rem(z + shift, RING)) * 2 + core_at
        level = dims[s] // GRAIN
        for sl in range(1, LEVELS + 1):

            @pl.when(level == sl)
            def _(sl=sl):
                inner = sl * GRAIN
                halves[s, :, :inner] = jnp.dot(
                    left[:, :inner], waves[slot, :inner, :inner], preferred_element_type=jnp.float32
                ).astype(jnp.bfloat16)
                if sl % 2:
                    halves[s, :, inner:inner + GRAIN] = jnp.zeros((left.shape[0], GRAIN), jnp.bfloat16)

        return carry

    lax.fori_loop(0, sectors, first_half, 0)
    for copy in right_copies:
        copy.wait()

    for kind in range(KINDS):
        inner = width if kind >= 2 else half
        cols = width if kind % 2 else half
        used = rows if kind % 2 else rows // 2

        def second_half(i, carry, inner=inner, cols=cols, used=used):
            for u in range(STEP):
                code = table[i * STEP + u]
                target = jnp.bitwise_and(code, 2 * sectors - 1)
                source = jnp.bitwise_and(lax.shift_right_logical(code, 5), sectors - 1)
                op = lax.shift_right_logical(code, 9)
                block = halves[source, pl.ds(pl.multiple_of(op * rows, rows), used), :inner]
                sums[target, :used, :cols] += jnp.dot(
                    block, right[op, :inner, :cols], preferred_element_type=jnp.float32
                )
            return carry

        lax.fori_loop(0 if kind == 0 else ends[kind - 1], ends[kind], second_half, 0)
    parts = out.shape[0]
    size = rows // parts
    column = lax.broadcasted_iota(jnp.int32, (size, width), 1)
    copies = []
    for part in range(parts):

        def finish(s, carry, part=part):
            limit = jnp.where(dims[s] > part * GRAIN, dims[s], 0)
            total = jnp.where(column < limit, sums[s, part * size:(part + 1) * size, :], 0.0)
            rounded[part, s] = total.astype(jnp.bfloat16)
            return carry

        lax.fori_loop(0, sectors, finish, 0)
        copy = pltpu.make_async_copy(rounded.at[part], out.at[part], out_sems.at[part])
        copy.start()
        copies.append(copy)
    for copy in copies:
        copy.wait()


def along_x(part, steps):
    return lax.ppermute(part, ("x_hi", "x_lo"), steps)


def to_mate(part):
    return lax.ppermute(part, "core", SWAP)


def share(block, left_ops, right_ops, meta):
    ops, width, _ = left_ops.shape
    half = width // 2
    rows = left_ops.reshape(ops, LEVELS, 2, 2, SLICE, width).transpose(2, 3, 0, 1, 4, 5)
    rows = rows.reshape(2, 2, ops * LEVELS * SLICE, width)
    y = lax.axis_index("y_lo")
    near_rows = lax.dynamic_index_in_dim(rows, y, 0, keepdims=False)
    sent_rows = lax.dynamic_index_in_dim(rows, 1 - y, 0, keepdims=False)
    far_right = lax.ppermute(right_ops, "y_lo", SWAP)
    far_rows = lax.ppermute(sent_rows, "y_lo", SWAP)
    before = lax.ppermute(block, "z", UP)
    after = lax.ppermute(block, "z", DOWN)
    side_low = along_x(block[:half], UP)
    side_high = along_x(block[half:], DOWN)
    across_low = lax.ppermute(before[:half], "z", UP)
    across_high = lax.ppermute(after[half:], "z", DOWN)
    side_before = along_x(before, UP)
    side_after = along_x(after, DOWN)
    corner_low = along_x(across_low, UP)
    corner_high = along_x(across_high, DOWN)
    metas = jnp.stack([meta, lax.ppermute(meta, "y_lo", SWAP)])
    metas = jnp.concatenate([metas, to_mate(metas)])
    early = (
        block, before, after, across_low, across_high, side_low, side_high, side_before, side_after,
    )
    own_waves = early + (corner_low, corner_high)
    held = lax.optimization_barrier(early + (right_ops, near_rows))
    mate_early = [to_mate(part) for part in held]
    mate_late = [to_mate(part) for part in (corner_low, corner_high, far_right, far_rows)]
    mate_waves = tuple(mate_early[:9] + mate_late[:2])
    operators = (right_ops, near_rows, mate_early[9], mate_early[10], far_right, far_rows, mate_late[2], mate_late[3])
    return own_waves + mate_waves + operators, metas


def body(
    wavefunction,
    left_ops,
    right_ops,
    sector_dims,
    coupling_source,
    coupling_target,
    coupling_operator,
):
    ops, width, _ = left_ops.shape
    sectors = 4 * RING
    meta = jnp.stack([coupling_source, coupling_target, coupling_operator])
    shared, metas = share(wavefunction[0], left_ops, right_ops, meta)
    y, core = lax.axis_index("y_lo"), lax.axis_index("core")
    owners = jnp.stack([2 * y + core, 2 * (1 - y) + core, 2 * y + 1 - core, 2 * (1 - y) + 1 - core])
    chosen = metas[:, 2] + ops * owners.astype(jnp.int32)[:, None]
    table, ends = plan_couplings(
        metas[:, 0].reshape(-1), metas[:, 1].reshape(-1), chosen.reshape(-1), sector_dims, width // 2
    )
    smem = pl.BlockSpec(memory_space=pltpu.SMEM)
    hbm = pl.BlockSpec(memory_space=pltpu.HBM)
    rows = width // GROUP
    partial = pl.pallas_call(
        couplings_kernel,
        out_shape=jax.ShapeDtypeStruct((LEVELS, sectors, SLICE, width), jnp.bfloat16),
        in_specs=[smem] * 3 + [hbm] * len(shared),
        out_specs=hbm,
        scratch_shapes=[
            pltpu.VMEM((ops * width, width), jnp.bfloat16),
            pltpu.VMEM((ops * GROUP, width, width), jnp.bfloat16),
            pltpu.VMEM((sectors, width, width), jnp.bfloat16),
            pltpu.VMEM((sectors, ops * width, width), jnp.bfloat16),
            pltpu.VMEM((sectors + 1, rows, width), jnp.float32),
            pltpu.VMEM((LEVELS, sectors, SLICE, width), jnp.bfloat16),
            pltpu.SemaphoreType.DMA((8,)),
            pltpu.SemaphoreType.DMA((sectors,)),
            pltpu.SemaphoreType.DMA((LEVELS,)),
        ],
        compiler_params=pltpu.CompilerParams(vmem_limit_bytes=56 * MIB),
        name="couplings",
    )(table, ends, sector_dims, *shared)
    got = lax.all_to_all(partial.reshape(-1, 2, SLICE, width), REDUCE, 0, 0, tiled=True)
    total = jnp.sum(got.astype(jnp.float32), axis=0).astype(jnp.bfloat16)
    spread = jnp.broadcast_to(total[None], (8,) + total.shape).reshape((16,) + total.shape[1:])
    whole = lax.all_to_all(spread, SPREAD, 0, 0, tiled=True)
    return whole.reshape(1, width, width).astype(jnp.float32)


def solution(mesh):
    fine = Mesh(mesh.devices.reshape(SIZES), AXES)
    everyone = P(AXES)
    placed = (
        P(SECTOR, None, None),
        P(AXES, None, None),
        P(AXES, None, None),
        P(),
        everyone,
        everyone,
        everyone,
    )
    return jax.shard_map(
        body, mesh=fine, in_specs=placed, out_specs=P(SECTOR, None, None), check_vma=False
    )
```

```python
import jax
import jax.numpy as jnp
from jax import lax
from jax.experimental import pallas as pl
from jax.experimental.pallas import tpu as pltpu
from jax.sharding import Mesh, PartitionSpec as P

AXES = ("x_hi", "y_hi", "y_lo", "x_lo", "z", "core")
SIZES = (2, 2, 2, 2, 4, 2)
SECTOR = ("x_lo", "z", "core")
REDUCE = ("x_hi", "y_lo", "x_lo", "z")
SPREAD = ("x_hi", "y_hi", "y_lo", "core")
RING = 4
GROUP = 4
LEVELS = 4
GRAIN = 128
SLICE = GRAIN // GROUP
STEP = 8
KINDS = 4
MIB = 1024 * 1024
SWAP = [(0, 1), (1, 0)]
UP = [(i, (i + 1) % RING) for i in range(RING)]
DOWN = [(i, (i - 1) % RING) for i in range(RING)]
SHIFTS = (0, RING - 1, 1, 2)


def plan_couplings(source, target, op, dims, half):
    sectors = dims.shape[0]
    count = source.shape[0]
    steps = (count + KINDS * (STEP - 1)) // STEP
    index = jnp.arange(sectors, dtype=jnp.int32)[None, :]
    wide = (dims > half).astype(jnp.int32)[None, :]
    wide_source = jnp.sum(jnp.where(source[:, None] == index, wide, 0), axis=1)
    wide_target = jnp.sum(jnp.where(target[:, None] == index, wide, 0), axis=1)
    kind = 2 * wide_source + wide_target
    kinds = jnp.arange(KINDS, dtype=jnp.int32)
    is_kind = kind[:, None] == kinds[None, :]
    taken = (jnp.sum(is_kind.astype(jnp.int32), axis=0) + STEP - 1) // STEP
    end = jnp.sum(jnp.where(kinds[:, None] <= kinds[None, :], taken[:, None], 0), axis=0)
    start = end - taken
    spot = jnp.arange(count, dtype=jnp.int32)
    earlier = (kind[:, None] == kind[None, :]) & (spot[:, None] < spot[None, :])
    rank = jnp.sum(earlier.astype(jnp.int32), axis=0)
    place = rank + STEP * jnp.sum(jnp.where(is_kind, start[None, :], 0), axis=1)
    here = place[:, None] == jnp.arange(steps * STEP, dtype=jnp.int32)[None, :]
    code = (op * sectors + source) * (2 * sectors) + target - sectors
    return sectors + jnp.sum(jnp.where(here, code[:, None], 0), axis=0), end


def couplings_kernel(table, ends, dims, *refs):
    own_waves, mate_waves = refs[:10], refs[10:20]
    own_right, own_left, mate_right, mate_left, far, far_mate = refs[20:26]
    out, left, right, waves, halves, sums, rounded, op_sems, wave_sems, out_sems = refs[26:]
    y, x, z, core = (lax.axis_index(name) for name in ("y_hi", "x_lo", "z", "core"))
    sectors, width, _ = waves.shape
    rows = sums.shape[1]
    ops = own_right.shape[0] // width
    half = width // 2
    left_copies, right_copies = [], []
    for n, (pair, c, left_rows, skip, right_ops) in enumerate((
        (y, core, own_left, 0, own_right),
        (y, 1 - core, mate_left, 0, mate_right),
        (1 - y, core, far, ops * width, far),
        (1 - y, 1 - core, far_mate, ops * width, far_mate),
    )):
        first = (pair * 2 + c) * ops
        size = ops * rows
        part = left_rows.at[pl.ds(pl.multiple_of(skip + core * size, size), size)]
        to = left.at[pl.ds(pl.multiple_of(first * rows, size), size)]
        left_copies.append(pltpu.make_async_copy(part, to, op_sems.at[2 * n]))
        part = right_ops.at[pl.ds(0, ops * width)]
        to = right.at[pl.ds(pl.multiple_of(first * width, ops * width), ops * width)]
        right_copies.append(pltpu.make_async_copy(part, to, op_sems.at[2 * n + 1]))
    for copy in left_copies:
        copy.start()
    whole, low, high = (pl.ds(0, width), pl.ds(0, half), pl.ds(half, half))
    places = (
        (0, whole), (1, whole), (2, whole), (3, low), (3, high),
        (4, whole), (5, whole), (6, whole), (7, low), (7, high),
    )
    for c, pieces in ((0, own_waves), (1, mate_waves)):
        for piece, (place, part) in zip(pieces, places):
            slot = c * (sectors // 2) + place
            pltpu.make_async_copy(piece, waves.at[slot, part], wave_sems.at[slot]).start()
    for copy in right_copies:
        copy.start()
    sums[...] = jnp.zeros_like(sums)
    for copy in left_copies:
        copy.wait()

    def first_half(slot, carry):
        pltpu.make_async_copy(waves.at[slot], waves.at[slot], wave_sems.at[slot]).wait()
        other_core = lax.div(slot, sectors // 2)
        other_x = lax.rem(lax.div(slot, RING), 2)
        step = lax.rem(slot, RING)
        shift = jnp.where(step == 1, RING - 1, jnp.where(step == 2, 1, jnp.where(step == 3, 2, 0)))
        x_at = lax.rem(x + other_x, 2)
        core_at = lax.rem(core + other_core, 2)
        s = (x_at * RING + lax.rem(z + shift, RING)) * 2 + core_at
        level = dims[s] // GRAIN
        for sl in range(1, LEVELS + 1):

            @pl.when(level == sl)
            def _(sl=sl):
                inner = sl * GRAIN
                halves[s, :, :inner] = jnp.dot(
                    left[:, :inner], waves[slot, :inner, :inner], preferred_element_type=jnp.float32
                ).astype(jnp.bfloat16)
                if sl % 2:
                    halves[s, :, inner:inner + GRAIN] = jnp.zeros((left.shape[0], GRAIN), jnp.bfloat16)

        return carry

    lax.fori_loop(0, sectors, first_half, 0)
    for copy in right_copies:
        copy.wait()

    for kind in range(KINDS):
        inner = width if kind >= 2 else half
        cols = width if kind % 2 else half
        used = rows if kind % 2 else rows // 2

        def second_half(i, carry, inner=inner, cols=cols, used=used):
            for u in range(STEP):
                code = table[i * STEP + u]
                target = jnp.bitwise_and(code, 2 * sectors - 1)
                source = jnp.bitwise_and(lax.shift_right_logical(code, 5), sectors - 1)
                op = lax.shift_right_logical(code, 9)
                block = halves[source, pl.ds(pl.multiple_of(op * rows, rows), used), :inner]
                sums[target, :used, :cols] += jnp.dot(
                    block,
                    right[pl.ds(pl.multiple_of(op * width, width), inner), :cols],
                    preferred_element_type=jnp.float32,
                )
            return carry

        lax.fori_loop(0 if kind == 0 else ends[kind - 1], ends[kind], second_half, 0)
    parts = out.shape[0]
    size = rows // parts
    column = lax.broadcasted_iota(jnp.int32, (size, width), 1)
    copies = []
    for part in range(parts):

        def finish(s, carry, part=part):
            limit = jnp.where(dims[s] > part * GRAIN, dims[s], 0)
            total = jnp.where(column < limit, sums[s, part * size:(part + 1) * size, :], 0.0)
            rounded[part, s] = total.astype(jnp.bfloat16)
            return carry

        lax.fori_loop(0, sectors, finish, 0)
        copy = pltpu.make_async_copy(rounded.at[part], out.at[part], out_sems.at[part])
        copy.start()
        copies.append(copy)
    for copy in copies:
        copy.wait()


def along_x(part, steps):
    return lax.ppermute(part, ("x_hi", "x_lo"), steps)


def to_mate(part):
    return lax.ppermute(part, "core", SWAP)


def share(block, left_ops, right_ops, meta):
    ops, width, _ = left_ops.shape
    half = width // 2
    size = ops * LEVELS * SLICE * 2
    rows = left_ops.reshape(ops, LEVELS, 2, 2, SLICE, width).transpose(2, 3, 0, 1, 4, 5)
    rows = rows.reshape(2, size, width)
    y = lax.axis_index("y_hi")
    near_rows = lax.dynamic_index_in_dim(rows, y, 0, keepdims=False)
    sent_rows = lax.dynamic_index_in_dim(rows, 1 - y, 0, keepdims=False)
    near_right = right_ops.reshape(ops * width, width)
    far = lax.ppermute(jnp.concatenate([near_right, sent_rows]), "y_hi", SWAP)
    before = lax.ppermute(block, "z", UP)
    after = lax.ppermute(block, "z", DOWN)
    side = along_x(block, UP)
    across_low = lax.ppermute(before[:half], "z", UP)
    across_high = lax.ppermute(after[half:], "z", DOWN)
    side_before = along_x(before, UP)
    side_after = along_x(after, DOWN)
    corner_low = along_x(across_low, UP)
    corner_high = along_x(across_high, DOWN)
    early = (block, before, after, across_low, across_high, side, side_before, side_after)
    held = lax.optimization_barrier(early + (near_right, near_rows))
    mate_early = [to_mate(part) for part in held]
    mate_late = [to_mate(part) for part in (corner_low, corner_high, far)]
    metas = jnp.stack([meta, lax.ppermute(meta, "y_hi", SWAP)])
    metas = jnp.concatenate([metas, to_mate(metas)])
    waves = early + (corner_low, corner_high) + tuple(mate_early[:8] + mate_late[:2])
    return waves + (near_right, near_rows, mate_early[8], mate_early[9], far, mate_late[2]), metas


def body(
    wavefunction,
    left_ops,
    right_ops,
    sector_dims,
    coupling_source,
    coupling_target,
    coupling_operator,
):
    ops, width, _ = left_ops.shape
    sectors = 4 * RING
    meta = jnp.stack([coupling_source, coupling_target, coupling_operator])
    shared, metas = share(wavefunction[0], left_ops, right_ops, meta)
    y, core = lax.axis_index("y_hi"), lax.axis_index("core")
    owners = jnp.stack([2 * y + core, 2 * (1 - y) + core, 2 * y + 1 - core, 2 * (1 - y) + 1 - core])
    chosen = metas[:, 2] + ops * owners.astype(jnp.int32)[:, None]
    table, ends = plan_couplings(
        metas[:, 0].reshape(-1), metas[:, 1].reshape(-1), chosen.reshape(-1), sector_dims, width // 2
    )
    smem = pl.BlockSpec(memory_space=pltpu.SMEM)
    hbm = pl.BlockSpec(memory_space=pltpu.HBM)
    rows = width // GROUP
    partial = pl.pallas_call(
        couplings_kernel,
        out_shape=jax.ShapeDtypeStruct((LEVELS, sectors, SLICE, width), jnp.bfloat16),
        in_specs=[smem] * 3 + [hbm] * len(shared),
        out_specs=hbm,
        scratch_shapes=[
            pltpu.VMEM((ops * width, width), jnp.bfloat16),
            pltpu.VMEM((ops * GROUP * width, width), jnp.bfloat16),
            pltpu.VMEM((sectors, width, width), jnp.bfloat16),
            pltpu.VMEM((sectors, ops * width, width), jnp.bfloat16),
            pltpu.VMEM((sectors + 1, rows, width), jnp.float32),
            pltpu.VMEM((LEVELS, sectors, SLICE, width), jnp.bfloat16),
            pltpu.SemaphoreType.DMA((8,)),
            pltpu.SemaphoreType.DMA((sectors,)),
            pltpu.SemaphoreType.DMA((LEVELS,)),
        ],
        compiler_params=pltpu.CompilerParams(vmem_limit_bytes=56 * MIB),
        name="couplings",
    )(table, ends, sector_dims, *shared)
    got = lax.all_to_all(partial.reshape(-1, 2, SLICE, width), REDUCE, 0, 0, tiled=True)
    total = jnp.sum(got.astype(jnp.float32), axis=0).astype(jnp.bfloat16)
    spread = jnp.broadcast_to(total[None], (8,) + total.shape).reshape((16,) + total.shape[1:])
    whole = lax.all_to_all(spread, SPREAD, 0, 0, tiled=True)
    whole = whole.reshape(2, 2, 2, 2, SLICE, width).transpose(0, 2, 1, 3, 4, 5)
    return whole.reshape(1, width, width).astype(jnp.float32)


def solution(mesh):
    fine = Mesh(mesh.devices.reshape(SIZES), AXES)
    everyone = P(AXES)
    placed = (
        P(SECTOR, None, None),
        P(AXES, None, None),
        P(AXES, None, None),
        P(),
        everyone,
        everyone,
        everyone,
    )
    return jax.shard_map(
        body, mesh=fine, in_specs=placed, out_specs=P(SECTOR, None, None), check_vma=False
    )
```

```python
import jax
import jax.numpy as jnp
from jax import lax
from jax.experimental import pallas as pl
from jax.experimental.pallas import tpu as pltpu
from jax.sharding import Mesh, PartitionSpec as P

AXES = ("x_hi", "y_hi", "y_lo", "x_lo", "z", "core")
SIZES = (2, 2, 2, 2, 4, 2)
SECTOR = ("x_lo", "z", "core")
REDUCE = ("x_hi", "y_lo", "x_lo", "z")
SPREAD = ("x_hi", "y_hi", "y_lo", "core")
RING = 4
GROUP = 4
LEVELS = 4
GRAIN = 128
SLICE = GRAIN // GROUP
STEP = 8
KINDS = 4
AHEAD = 4
MIB = 1024 * 1024
SWAP = [(0, 1), (1, 0)]
UP = [(i, (i + 1) % RING) for i in range(RING)]
DOWN = [(i, (i - 1) % RING) for i in range(RING)]
SHIFTS = (0, RING - 1, 1, 2)


def plan_couplings(source, target, op, dims, half):
    sectors = dims.shape[0]
    count = source.shape[0]
    steps = (count + KINDS * (STEP - 1)) // STEP
    index = jnp.arange(sectors, dtype=jnp.int32)[None, :]
    wide = (dims > half).astype(jnp.int32)[None, :]
    wide_source = jnp.sum(jnp.where(source[:, None] == index, wide, 0), axis=1)
    wide_target = jnp.sum(jnp.where(target[:, None] == index, wide, 0), axis=1)
    kind = 2 * wide_source + wide_target
    kinds = jnp.arange(KINDS, dtype=jnp.int32)
    is_kind = kind[:, None] == kinds[None, :]
    taken = (jnp.sum(is_kind.astype(jnp.int32), axis=0) + STEP - 1) // STEP
    end = jnp.sum(jnp.where(kinds[:, None] <= kinds[None, :], taken[:, None], 0), axis=0)
    start = end - taken
    spot = jnp.arange(count, dtype=jnp.int32)
    earlier = (kind[:, None] == kind[None, :]) & (spot[:, None] < spot[None, :])
    rank = jnp.sum(earlier.astype(jnp.int32), axis=0)
    place = rank + STEP * jnp.sum(jnp.where(is_kind, start[None, :], 0), axis=1)
    here = place[:, None] == jnp.arange(steps * STEP, dtype=jnp.int32)[None, :]
    code = (op * sectors + source) * (2 * sectors) + target - sectors
    return sectors + jnp.sum(jnp.where(here, code[:, None], 0), axis=0), end


def couplings_kernel(table, ends, dims, *refs):
    own_waves, mate_waves = refs[:10], refs[10:20]
    own_right, own_left, mate_right, mate_left, far, far_mate = refs[20:26]
    out, left, right, waves, halves, sums, rounded, op_sems, wave_sems, out_sems = refs[26:]
    y, x, z, core = (lax.axis_index(name) for name in ("y_hi", "x_lo", "z", "core"))
    sectors, width, _ = waves.shape
    rows = sums.shape[1]
    ops = own_right.shape[0] // width
    half = width // 2
    left_copies, right_copies = [], []
    for n, (pair, c, left_rows, skip, right_ops) in enumerate((
        (y, core, own_left, 0, own_right),
        (y, 1 - core, mate_left, 0, mate_right),
        (1 - y, core, far, ops * width, far),
        (1 - y, 1 - core, far_mate, ops * width, far_mate),
    )):
        first = (pair * 2 + c) * ops
        size = ops * rows
        part = left_rows.at[pl.ds(pl.multiple_of(skip + core * size, size), size)]
        to = left.at[pl.ds(pl.multiple_of(first * rows, size), size)]
        left_copies.append(pltpu.make_async_copy(part, to, op_sems.at[2 * n]))
        part = right_ops.at[pl.ds(0, ops * width)]
        to = right.at[pl.ds(pl.multiple_of(first * width, ops * width), ops * width)]
        right_copies.append(pltpu.make_async_copy(part, to, op_sems.at[2 * n + 1]))
    for copy in left_copies:
        copy.start()
    whole, low, high = (pl.ds(0, width), pl.ds(0, half), pl.ds(half, half))
    places = (
        (0, whole), (1, whole), (2, whole), (3, low), (3, high),
        (4, whole), (5, whole), (6, whole), (7, low), (7, high),
    )
    wave_copies = [[] for _ in range(sectors)]
    for c, pieces in ((0, own_waves), (1, mate_waves)):
        for piece, (place, part) in zip(pieces, places):
            slot = c * (sectors // 2) + place
            wave_copies[slot].append(pltpu.make_async_copy(piece, waves.at[slot, part], wave_sems.at[slot]))
    for slot in range(AHEAD):
        for copy in wave_copies[slot]:
            copy.start()
    sums[...] = jnp.zeros_like(sums)
    for copy in left_copies:
        copy.wait()

    def first_half(slot, carry):
        for later in range(AHEAD, sectors):

            @pl.when(slot == later - AHEAD)
            def _(later=later):
                for copy in wave_copies[later]:
                    copy.start()

        @pl.when(slot == sectors - AHEAD)
        def _():
            for copy in right_copies:
                copy.start()

        pltpu.make_async_copy(waves.at[slot], waves.at[slot], wave_sems.at[slot]).wait()
        other_core = lax.div(slot, sectors // 2)
        other_x = lax.rem(lax.div(slot, RING), 2)
        step = lax.rem(slot, RING)
        shift = jnp.where(step == 1, RING - 1, jnp.where(step == 2, 1, jnp.where(step == 3, 2, 0)))
        x_at = lax.rem(x + other_x, 2)
        core_at = lax.rem(core + other_core, 2)
        s = (x_at * RING + lax.rem(z + shift, RING)) * 2 + core_at
        level = dims[s] // GRAIN
        for sl in range(1, LEVELS + 1):

            @pl.when(level == sl)
            def _(sl=sl):
                inner = sl * GRAIN
                halves[s, :, :inner] = jnp.dot(
                    left[:, :inner], waves[slot, :inner, :inner], preferred_element_type=jnp.float32
                ).astype(jnp.bfloat16)
                if sl % 2:
                    halves[s, :, inner:inner + GRAIN] = jnp.zeros((left.shape[0], GRAIN), jnp.bfloat16)

        return carry

    lax.fori_loop(0, sectors, first_half, 0)
    for copy in right_copies:
        copy.wait()

    for kind in range(KINDS):
        inner = width if kind >= 2 else half
        cols = width if kind % 2 else half
        used = rows if kind % 2 else rows // 2

        def second_half(i, carry, inner=inner, cols=cols, used=used):
            for u in range(STEP):
                code = table[i * STEP + u]
                target = jnp.bitwise_and(code, 2 * sectors - 1)
                source = jnp.bitwise_and(lax.shift_right_logical(code, 5), sectors - 1)
                op = lax.shift_right_logical(code, 9)
                block = halves[source, pl.ds(pl.multiple_of(op * rows, rows), used), :inner]
                sums[target, :used, :cols] += jnp.dot(
                    block,
                    right[pl.ds(pl.multiple_of(op * width, width), inner), :cols],
                    preferred_element_type=jnp.float32,
                )
            return carry

        lax.fori_loop(0 if kind == 0 else ends[kind - 1], ends[kind], second_half, 0)
    parts = out.shape[0]
    size = rows // parts
    column = lax.broadcasted_iota(jnp.int32, (size, width), 1)
    copies = []
    for part in range(parts):

        def finish(s, carry, part=part):
            limit = jnp.where(dims[s] > part * GRAIN, dims[s], 0)
            total = jnp.where(column < limit, sums[s, part * size:(part + 1) * size, :], 0.0)
            rounded[part, s] = total.astype(jnp.bfloat16)
            return carry

        lax.fori_loop(0, sectors, finish, 0)
        copy = pltpu.make_async_copy(rounded.at[part], out.at[part], out_sems.at[part])
        copy.start()
        copies.append(copy)
    for copy in copies:
        copy.wait()


def along_x(part, steps):
    return lax.ppermute(part, ("x_hi", "x_lo"), steps)


def to_mate(part):
    return lax.ppermute(part, "core", SWAP)


def share(block, left_ops, right_ops, meta):
    ops, width, _ = left_ops.shape
    half = width // 2
    size = ops * LEVELS * SLICE * 2
    rows = left_ops.reshape(ops, LEVELS, 2, 2, SLICE, width).transpose(2, 3, 0, 1, 4, 5)
    rows = rows.reshape(2, size, width)
    y = lax.axis_index("y_hi")
    near_rows = lax.dynamic_index_in_dim(rows, y, 0, keepdims=False)
    sent_rows = lax.dynamic_index_in_dim(rows, 1 - y, 0, keepdims=False)
    near_right = right_ops.reshape(ops * width, width)
    far_meta = lax.ppermute(meta, "y_hi", SWAP)
    sent_right, sent_rows, far_meta = lax.optimization_barrier((near_right, sent_rows, far_meta))
    far = lax.ppermute(jnp.concatenate([sent_right, sent_rows]), "y_hi", SWAP)
    before = lax.ppermute(block, "z", UP)
    after = lax.ppermute(block, "z", DOWN)
    side = along_x(block, UP)
    across_low = lax.ppermute(before[:half], "z", UP)
    across_high = lax.ppermute(after[half:], "z", DOWN)
    side_before = along_x(before, UP)
    side_after = along_x(after, DOWN)
    corner_low = along_x(across_low, UP)
    corner_high = along_x(across_high, DOWN)
    early = (block, before, after, across_low, across_high, side, side_before, side_after)
    held = lax.optimization_barrier(early + (near_right, near_rows))
    mate_early = [to_mate(part) for part in held]
    mate_late = [to_mate(part) for part in (corner_low, corner_high, far)]
    metas = jnp.stack([meta, far_meta])
    metas, _ = lax.optimization_barrier((metas, held[6]))
    metas = jnp.concatenate([metas, to_mate(metas)])
    waves = early + (corner_low, corner_high) + tuple(mate_early[:8] + mate_late[:2])
    return waves + (near_right, near_rows, mate_early[8], mate_early[9], far, mate_late[2]), metas


def body(
    wavefunction,
    left_ops,
    right_ops,
    sector_dims,
    coupling_source,
    coupling_target,
    coupling_operator,
):
    ops, width, _ = left_ops.shape
    sectors = 4 * RING
    meta = jnp.stack([coupling_source, coupling_target, coupling_operator])
    shared, metas = share(wavefunction[0], left_ops, right_ops, meta)
    y, core = lax.axis_index("y_hi"), lax.axis_index("core")
    owners = jnp.stack([2 * y + core, 2 * (1 - y) + core, 2 * y + 1 - core, 2 * (1 - y) + 1 - core])
    chosen = metas[:, 2] + ops * owners.astype(jnp.int32)[:, None]
    table, ends = plan_couplings(
        metas[:, 0].reshape(-1), metas[:, 1].reshape(-1), chosen.reshape(-1), sector_dims, width // 2
    )
    smem = pl.BlockSpec(memory_space=pltpu.SMEM)
    hbm = pl.BlockSpec(memory_space=pltpu.HBM)
    rows = width // GROUP
    partial = pl.pallas_call(
        couplings_kernel,
        out_shape=jax.ShapeDtypeStruct((LEVELS, sectors, SLICE, width), jnp.bfloat16),
        in_specs=[smem] * 3 + [hbm] * len(shared),
        out_specs=hbm,
        scratch_shapes=[
            pltpu.VMEM((ops * width, width), jnp.bfloat16),
            pltpu.VMEM((ops * GROUP * width, width), jnp.bfloat16),
            pltpu.VMEM((sectors, width, width), jnp.bfloat16),
            pltpu.VMEM((sectors, ops * width, width), jnp.bfloat16),
            pltpu.VMEM((sectors + 1, rows, width), jnp.float32),
            pltpu.VMEM((LEVELS, sectors, SLICE, width), jnp.bfloat16),
            pltpu.SemaphoreType.DMA((8,)),
            pltpu.SemaphoreType.DMA((sectors,)),
            pltpu.SemaphoreType.DMA((LEVELS,)),
        ],
        compiler_params=pltpu.CompilerParams(vmem_limit_bytes=56 * MIB),
        name="couplings",
    )(table, ends, sector_dims, *shared)
    got = lax.all_to_all(partial.reshape(-1, 2, SLICE, width), REDUCE, 0, 0, tiled=True)
    total = jnp.sum(got.astype(jnp.float32), axis=0).astype(jnp.bfloat16)
    spread = jnp.broadcast_to(total[None], (8,) + total.shape).reshape((16,) + total.shape[1:])
    whole = lax.all_to_all(spread, SPREAD, 0, 0, tiled=True)
    whole = whole.reshape(2, 2, 2, 2, SLICE, width).transpose(0, 2, 1, 3, 4, 5)
    return whole.reshape(1, width, width).astype(jnp.float32)


def solution(mesh):
    fine = Mesh(mesh.devices.reshape(SIZES), AXES)
    everyone = P(AXES)
    placed = (
        P(SECTOR, None, None),
        P(AXES, None, None),
        P(AXES, None, None),
        P(),
        everyone,
        everyone,
        everyone,
    )
    return jax.shard_map(
        body, mesh=fine, in_specs=placed, out_specs=P(SECTOR, None, None), check_vma=False
    )
```

```python
import jax
import jax.numpy as jnp
from jax import lax
from jax.experimental import pallas as pl
from jax.experimental.pallas import tpu as pltpu
from jax.sharding import Mesh, PartitionSpec as P

AXES = ("x_hi", "y_hi", "y_lo", "x_lo", "z", "core")
SIZES = (2, 2, 2, 2, 4, 2)
SECTOR = ("x_lo", "z", "core")
REDUCE = ("x_hi", "y_lo", "x_lo", "z")
SPREAD = ("x_hi", "y_hi", "y_lo", "core")
RING = 4
GROUP = 4
LEVELS = 4
GRAIN = 128
SLICE = GRAIN // GROUP
STEP = 8
KINDS = 4
AHEAD = 4
MIB = 1024 * 1024
SWAP = [(0, 1), (1, 0)]
UP = [(i, (i + 1) % RING) for i in range(RING)]
DOWN = [(i, (i - 1) % RING) for i in range(RING)]
SHIFTS = (0, RING - 1, 1, 2)


def plan_couplings(source, target, op, dims, half):
    sectors = dims.shape[0]
    count = source.shape[0]
    steps = (count + KINDS * (STEP - 1)) // STEP
    index = jnp.arange(sectors, dtype=jnp.int32)[None, :]
    wide = (dims > half).astype(jnp.int32)[None, :]
    wide_source = jnp.sum(jnp.where(source[:, None] == index, wide, 0), axis=1)
    wide_target = jnp.sum(jnp.where(target[:, None] == index, wide, 0), axis=1)
    kind = 2 * wide_source + wide_target
    kinds = jnp.arange(KINDS, dtype=jnp.int32)
    is_kind = kind[:, None] == kinds[None, :]
    taken = (jnp.sum(is_kind.astype(jnp.int32), axis=0) + STEP - 1) // STEP
    end = jnp.sum(jnp.where(kinds[:, None] <= kinds[None, :], taken[:, None], 0), axis=0)
    start = end - taken
    spot = jnp.arange(count, dtype=jnp.int32)
    earlier = (kind[:, None] == kind[None, :]) & (spot[:, None] < spot[None, :])
    rank = jnp.sum(earlier.astype(jnp.int32), axis=0)
    place = rank + STEP * jnp.sum(jnp.where(is_kind, start[None, :], 0), axis=1)
    here = place[:, None] == jnp.arange(steps * STEP, dtype=jnp.int32)[None, :]
    code = (op * sectors + source) * (2 * sectors) + target - sectors
    return sectors + jnp.sum(jnp.where(here, code[:, None], 0), axis=0), end


def couplings_kernel(table, ends, dims, *refs):
    own_waves, mate_waves = refs[:10], refs[10:20]
    own_right, own_left, mate_right, mate_left, far, far_mate = refs[20:26]
    out, left, right, waves, halves, sums, rounded, op_sems, wave_sems, out_sems = refs[26:]
    y, x, z, core = (lax.axis_index(name) for name in ("y_hi", "x_lo", "z", "core"))
    sectors, width, _ = waves.shape
    rows = sums.shape[1]
    ops = own_right.shape[0] // width
    half = width // 2
    left_copies, right_copies = [], []
    for n, (pair, c, left_rows, skip, right_ops) in enumerate((
        (y, core, own_left, 0, own_right),
        (y, 1 - core, mate_left, 0, mate_right),
        (1 - y, core, far, ops * width, far),
        (1 - y, 1 - core, far_mate, ops * width, far_mate),
    )):
        first = (pair * 2 + c) * ops
        size = ops * rows
        part = left_rows.at[pl.ds(pl.multiple_of(skip + core * size, size), size)]
        to = left.at[pl.ds(pl.multiple_of(first * rows, size), size)]
        left_copies.append(pltpu.make_async_copy(part, to, op_sems.at[2 * n]))
        part = right_ops.at[pl.ds(0, ops * width)]
        to = right.at[pl.ds(pl.multiple_of(first * width, ops * width), ops * width)]
        right_copies.append(pltpu.make_async_copy(part, to, op_sems.at[2 * n + 1]))
    for copy in left_copies:
        copy.start()
    whole, low, high = (pl.ds(0, width), pl.ds(0, half), pl.ds(half, half))
    places = (
        (0, whole), (1, whole), (2, whole), (3, low), (3, high),
        (4, whole), (5, whole), (6, whole), (7, low), (7, high),
    )
    wave_copies = [[] for _ in range(sectors)]
    for c, pieces in ((0, own_waves), (1, mate_waves)):
        for piece, (place, part) in zip(pieces, places):
            slot = c * (sectors // 2) + place
            wave_copies[slot].append(pltpu.make_async_copy(piece, waves.at[slot, part], wave_sems.at[slot]))
    for slot in range(AHEAD):
        for copy in wave_copies[slot]:
            copy.start()
    sums[...] = jnp.zeros_like(sums)
    for copy in left_copies:
        copy.wait()

    def first_half(slot, carry):
        for later in range(AHEAD, sectors):

            @pl.when(slot == later - AHEAD)
            def _(later=later):
                for copy in wave_copies[later]:
                    copy.start()

        @pl.when(slot == sectors - AHEAD)
        def _():
            for copy in right_copies:
                copy.start()

        pltpu.make_async_copy(waves.at[slot], waves.at[slot], wave_sems.at[slot]).wait()
        other_core = lax.div(slot, sectors // 2)
        other_x = lax.rem(lax.div(slot, RING), 2)
        step = lax.rem(slot, RING)
        shift = jnp.where(step == 1, RING - 1, jnp.where(step == 2, 1, jnp.where(step == 3, 2, 0)))
        x_at = lax.rem(x + other_x, 2)
        core_at = lax.rem(core + other_core, 2)
        s = (x_at * RING + lax.rem(z + shift, RING)) * 2 + core_at
        level = dims[s] // GRAIN
        for sl in range(1, LEVELS + 1):

            @pl.when(level == sl)
            def _(sl=sl):
                inner = sl * GRAIN
                halves[s, :, :inner] = jnp.dot(
                    left[:, :inner], waves[slot, :inner, :inner], preferred_element_type=jnp.float32
                ).astype(jnp.bfloat16)
                if sl % 2:
                    halves[s, :, inner:inner + GRAIN] = jnp.zeros((left.shape[0], GRAIN), jnp.bfloat16)

        return carry

    lax.fori_loop(0, sectors, first_half, 0)
    for copy in right_copies:
        copy.wait()

    for kind in range(KINDS):
        inner = width if kind >= 2 else half
        cols = width if kind % 2 else half
        used = rows if kind % 2 else rows // 2

        def second_half(i, carry, inner=inner, cols=cols, used=used):
            for u in range(STEP):
                code = table[i * STEP + u]
                target = jnp.bitwise_and(code, 2 * sectors - 1)
                source = jnp.bitwise_and(lax.shift_right_logical(code, 5), sectors - 1)
                op = lax.shift_right_logical(code, 9)
                block = halves[source, pl.ds(pl.multiple_of(op * rows, rows), used), :inner]
                sums[target, :used, :cols] += jnp.dot(
                    block,
                    right[pl.ds(pl.multiple_of(op * width, width), inner), :cols],
                    preferred_element_type=jnp.float32,
                )
            return carry

        lax.fori_loop(0 if kind == 0 else ends[kind - 1], ends[kind], second_half, 0)
    parts = out.shape[0]
    size = rows // parts
    column = lax.broadcasted_iota(jnp.int32, (size, width), 1)
    copies = []
    for part in range(parts):

        def finish(s, carry, part=part):
            limit = jnp.where(dims[s] > part * GRAIN, dims[s], 0)
            total = jnp.where(column < limit, sums[s, part * size:(part + 1) * size, :], 0.0)
            rounded[part, s] = total.astype(jnp.bfloat16)
            return carry

        lax.fori_loop(0, sectors, finish, 0)
        copy = pltpu.make_async_copy(rounded.at[part], out.at[part], out_sems.at[part])
        copy.start()
        copies.append(copy)
    for copy in copies:
        copy.wait()


def along_x(part, steps):
    return lax.ppermute(part, ("x_hi", "x_lo"), steps)


def to_mate(part):
    return lax.ppermute(part, "core", SWAP)


def share(block, left_ops, right_ops, meta):
    ops, width, _ = left_ops.shape
    half = width // 2
    size = ops * LEVELS * SLICE * 2
    rows = left_ops.reshape(ops, LEVELS, 2, 2, SLICE, width).transpose(2, 3, 0, 1, 4, 5)
    rows = rows.reshape(2, size, width)
    y = lax.axis_index("y_hi")
    near_rows = lax.dynamic_index_in_dim(rows, y, 0, keepdims=False)
    sent_rows = lax.dynamic_index_in_dim(rows, 1 - y, 0, keepdims=False)
    near_right = right_ops.reshape(ops * width, width)
    far_meta = lax.ppermute(meta, "y_hi", SWAP)
    sent_right, sent_rows, far_meta = lax.optimization_barrier((near_right, sent_rows, far_meta))
    far = lax.ppermute(jnp.concatenate([sent_right, sent_rows]), "y_hi", SWAP)
    before = lax.ppermute(block, "z", UP)
    after = lax.ppermute(block, "z", DOWN)
    side = along_x(block, UP)
    across_low = lax.ppermute(before[:half], "z", UP)
    across_high = lax.ppermute(after[half:], "z", DOWN)
    side_before = along_x(before, UP)
    side_after = along_x(after, DOWN)
    corner_low = along_x(across_low, UP)
    corner_high = along_x(across_high, DOWN)
    early = (block, before, after, across_low, across_high, side, side_before, side_after)
    first = tuple(to_mate(part) for part in (block, near_right, near_rows))
    held = lax.optimization_barrier(early + first)
    mate_early = [held[8]] + [to_mate(part) for part in held[1:8]] + list(held[9:])
    mate_late = [to_mate(part) for part in (corner_low, corner_high, far)]
    metas = jnp.stack([meta, far_meta])
    metas, _ = lax.optimization_barrier((metas, held[6]))
    metas = jnp.concatenate([metas, to_mate(metas)])
    waves = early + (corner_low, corner_high) + tuple(mate_early[:8] + mate_late[:2])
    return waves + (near_right, near_rows, mate_early[8], mate_early[9], far, mate_late[2]), metas


def body(
    wavefunction,
    left_ops,
    right_ops,
    sector_dims,
    coupling_source,
    coupling_target,
    coupling_operator,
):
    ops, width, _ = left_ops.shape
    sectors = 4 * RING
    meta = jnp.stack([coupling_source, coupling_target, coupling_operator])
    shared, metas = share(wavefunction[0], left_ops, right_ops, meta)
    y, core = lax.axis_index("y_hi"), lax.axis_index("core")
    owners = jnp.stack([2 * y + core, 2 * (1 - y) + core, 2 * y + 1 - core, 2 * (1 - y) + 1 - core])
    chosen = metas[:, 2] + ops * owners.astype(jnp.int32)[:, None]
    table, ends = plan_couplings(
        metas[:, 0].reshape(-1), metas[:, 1].reshape(-1), chosen.reshape(-1), sector_dims, width // 2
    )
    smem = pl.BlockSpec(memory_space=pltpu.SMEM)
    hbm = pl.BlockSpec(memory_space=pltpu.HBM)
    rows = width // GROUP
    partial = pl.pallas_call(
        couplings_kernel,
        out_shape=jax.ShapeDtypeStruct((LEVELS, sectors, SLICE, width), jnp.bfloat16),
        in_specs=[smem] * 3 + [hbm] * len(shared),
        out_specs=hbm,
        scratch_shapes=[
            pltpu.VMEM((ops * width, width), jnp.bfloat16),
            pltpu.VMEM((ops * GROUP * width, width), jnp.bfloat16),
            pltpu.VMEM((sectors, width, width), jnp.bfloat16),
            pltpu.VMEM((sectors, ops * width, width), jnp.bfloat16),
            pltpu.VMEM((sectors + 1, rows, width), jnp.float32),
            pltpu.VMEM((LEVELS, sectors, SLICE, width), jnp.bfloat16),
            pltpu.SemaphoreType.DMA((8,)),
            pltpu.SemaphoreType.DMA((sectors,)),
            pltpu.SemaphoreType.DMA((LEVELS,)),
        ],
        compiler_params=pltpu.CompilerParams(vmem_limit_bytes=56 * MIB),
        name="couplings",
    )(table, ends, sector_dims, *shared)
    got = lax.all_to_all(partial.reshape(-1, 2, SLICE, width), REDUCE, 0, 0, tiled=True)
    total = jnp.sum(got.astype(jnp.float32), axis=0).astype(jnp.bfloat16)
    spread = jnp.broadcast_to(total[None], (8,) + total.shape).reshape((16,) + total.shape[1:])
    whole = lax.all_to_all(spread, SPREAD, 0, 0, tiled=True)
    whole = whole.reshape(2, 2, 2, 2, SLICE, width).transpose(0, 2, 1, 3, 4, 5)
    return whole.reshape(1, width, width).astype(jnp.float32)


def solution(mesh):
    fine = Mesh(mesh.devices.reshape(SIZES), AXES)
    everyone = P(AXES)
    placed = (
        P(SECTOR, None, None),
        P(AXES, None, None),
        P(AXES, None, None),
        P(),
        everyone,
        everyone,
        everyone,
    )
    return jax.shard_map(
        body, mesh=fine, in_specs=placed, out_specs=P(SECTOR, None, None), check_vma=False
    )
```

```python
import jax
import jax.numpy as jnp
from jax import lax
from jax.experimental import pallas as pl
from jax.experimental.pallas import tpu as pltpu
from jax.sharding import Mesh, PartitionSpec as P

AXES = ("x_hi", "y_hi", "y_lo", "x_lo", "z", "core")
SIZES = (2, 2, 2, 2, 4, 2)
SECTOR = ("x_lo", "z", "core")
REDUCE = ("x_hi", "y_lo", "x_lo", "z")
SPREAD = ("x_hi", "y_hi", "y_lo", "core")
RING = 4
GROUP = 4
LEVELS = 4
GRAIN = 128
SLICE = GRAIN // GROUP
STEP = 8
KINDS = 4
AHEAD = 4
MIB = 1024 * 1024
SWAP = [(0, 1), (1, 0)]
UP = [(i, (i + 1) % RING) for i in range(RING)]
DOWN = [(i, (i - 1) % RING) for i in range(RING)]
SHIFTS = (0, RING - 1, 1, 2)


def plan_couplings(source, target, op, dims, half):
    sectors = dims.shape[0]
    count = source.shape[0]
    steps = (count + KINDS * (STEP - 1)) // STEP
    index = jnp.arange(sectors, dtype=jnp.int32)[None, :]
    wide = (dims > half).astype(jnp.int32)[None, :]
    wide_source = jnp.sum(jnp.where(source[:, None] == index, wide, 0), axis=1)
    wide_target = jnp.sum(jnp.where(target[:, None] == index, wide, 0), axis=1)
    kind = 2 * wide_source + wide_target
    kinds = jnp.arange(KINDS, dtype=jnp.int32)
    is_kind = kind[:, None] == kinds[None, :]
    taken = (jnp.sum(is_kind.astype(jnp.int32), axis=0) + STEP - 1) // STEP
    end = jnp.sum(jnp.where(kinds[:, None] <= kinds[None, :], taken[:, None], 0), axis=0)
    start = end - taken
    spot = jnp.arange(count, dtype=jnp.int32)
    earlier = (kind[:, None] == kind[None, :]) & (spot[:, None] < spot[None, :])
    rank = jnp.sum(earlier.astype(jnp.int32), axis=0)
    place = rank + STEP * jnp.sum(jnp.where(is_kind, start[None, :], 0), axis=1)
    here = place[:, None] == jnp.arange(steps * STEP, dtype=jnp.int32)[None, :]
    code = (op * sectors + source) * (2 * sectors) + target - sectors
    return sectors + jnp.sum(jnp.where(here, code[:, None], 0), axis=0), end


def couplings_kernel(table, ends, dims, *refs):
    own_waves, mate_waves = refs[:10], refs[10:20]
    own_right, own_left, mate_right, mate_left, far_right, far_left, far_mate_right, far_mate_left = refs[20:28]
    out, left, right, waves, halves, sums, rounded, op_sems, wave_sems, out_sems = refs[28:]
    y, x, z, core = (lax.axis_index(name) for name in ("y_hi", "x_lo", "z", "core"))
    sectors, width, _ = waves.shape
    rows = sums.shape[1]
    ops = own_right.shape[0] // width
    half = width // 2
    left_copies, right_copies = [], []
    for n, (pair, c, left_rows, right_ops) in enumerate((
        (y, core, own_left, own_right),
        (y, 1 - core, mate_left, mate_right),
        (1 - y, core, far_left, far_right),
        (1 - y, 1 - core, far_mate_left, far_mate_right),
    )):
        first = (pair * 2 + c) * ops
        size = ops * rows
        part = left_rows.at[pl.ds(pl.multiple_of(core * size, size), size)]
        to = left.at[pl.ds(pl.multiple_of(first * rows, size), size)]
        left_copies.append(pltpu.make_async_copy(part, to, op_sems.at[2 * n]))
        to = right.at[pl.ds(pl.multiple_of(first * width, ops * width), ops * width)]
        right_copies.append(pltpu.make_async_copy(right_ops, to, op_sems.at[2 * n + 1]))
    for copy in left_copies:
        copy.start()
    whole, low, high = (pl.ds(0, width), pl.ds(0, half), pl.ds(half, half))
    places = (
        (0, whole), (1, whole), (2, whole), (3, low), (3, high),
        (4, whole), (5, whole), (6, whole), (7, low), (7, high),
    )
    wave_copies = [[] for _ in range(sectors)]
    for c, pieces in ((0, own_waves), (1, mate_waves)):
        for piece, (place, part) in zip(pieces, places):
            slot = c * (sectors // 2) + place
            wave_copies[slot].append(pltpu.make_async_copy(piece, waves.at[slot, part], wave_sems.at[slot]))
    for slot in range(AHEAD):
        for copy in wave_copies[slot]:
            copy.start()
    sums[...] = jnp.zeros_like(sums)
    for copy in left_copies:
        copy.wait()

    def first_half(slot, carry):
        for later in range(AHEAD, sectors):

            @pl.when(slot == later - AHEAD)
            def _(later=later):
                for copy in wave_copies[later]:
                    copy.start()

        @pl.when(slot == sectors - AHEAD)
        def _():
            for copy in right_copies:
                copy.start()

        pltpu.make_async_copy(waves.at[slot], waves.at[slot], wave_sems.at[slot]).wait()
        other_core = lax.div(slot, sectors // 2)
        other_x = lax.rem(lax.div(slot, RING), 2)
        step = lax.rem(slot, RING)
        shift = jnp.where(step == 1, RING - 1, jnp.where(step == 2, 1, jnp.where(step == 3, 2, 0)))
        x_at = lax.rem(x + other_x, 2)
        core_at = lax.rem(core + other_core, 2)
        s = (x_at * RING + lax.rem(z + shift, RING)) * 2 + core_at
        level = dims[s] // GRAIN
        for sl in range(1, LEVELS + 1):

            @pl.when(level == sl)
            def _(sl=sl):
                inner = sl * GRAIN
                halves[s, :, :inner] = jnp.dot(
                    left[:, :inner], waves[slot, :inner, :inner], preferred_element_type=jnp.float32
                ).astype(jnp.bfloat16)
                if sl % 2:
                    halves[s, :, inner:inner + GRAIN] = jnp.zeros((left.shape[0], GRAIN), jnp.bfloat16)

        return carry

    lax.fori_loop(0, sectors, first_half, 0)
    for copy in right_copies:
        copy.wait()

    for kind in range(KINDS):
        inner = width if kind >= 2 else half
        cols = width if kind % 2 else half
        used = rows if kind % 2 else rows // 2

        def second_half(i, carry, inner=inner, cols=cols, used=used):
            for u in range(STEP):
                code = table[i * STEP + u]
                target = jnp.bitwise_and(code, 2 * sectors - 1)
                source = jnp.bitwise_and(lax.shift_right_logical(code, 5), sectors - 1)
                op = lax.shift_right_logical(code, 9)
                block = halves[source, pl.ds(pl.multiple_of(op * rows, rows), used), :inner]
                sums[target, :used, :cols] += jnp.dot(
                    block,
                    right[pl.ds(pl.multiple_of(op * width, width), inner), :cols],
                    preferred_element_type=jnp.float32,
                )
            return carry

        lax.fori_loop(0 if kind == 0 else ends[kind - 1], ends[kind], second_half, 0)
    parts = out.shape[0]
    size = rows // parts
    column = lax.broadcasted_iota(jnp.int32, (size, width), 1)
    copies = []
    for part in range(parts):

        def finish(s, carry, part=part):
            limit = jnp.where(dims[s] > part * GRAIN, dims[s], 0)
            total = jnp.where(column < limit, sums[s, part * size:(part + 1) * size, :], 0.0)
            rounded[part, s] = total.astype(jnp.bfloat16)
            return carry

        lax.fori_loop(0, sectors, finish, 0)
        copy = pltpu.make_async_copy(rounded.at[part], out.at[part], out_sems.at[part])
        copy.start()
        copies.append(copy)
    for copy in copies:
        copy.wait()


def along_x(part, steps):
    return lax.ppermute(part, ("x_hi", "x_lo"), steps)


def to_mate(part):
    return lax.ppermute(part, "core", SWAP)


def share(block, left_ops, right_ops, meta):
    ops, width, _ = left_ops.shape
    half = width // 2
    size = ops * LEVELS * SLICE * 2
    rows = left_ops.reshape(ops, LEVELS, 2, 2, SLICE, width).transpose(2, 3, 0, 1, 4, 5)
    rows = rows.reshape(2, size, width)
    y = lax.axis_index("y_hi")
    near_rows = lax.dynamic_index_in_dim(rows, y, 0, keepdims=False)
    sent_rows = lax.dynamic_index_in_dim(rows, 1 - y, 0, keepdims=False)
    near_right = right_ops.reshape(ops * width, width)
    lists = jnp.pad(meta.astype(jnp.bfloat16), ((0, 16 - meta.shape[0]), (0, width - meta.shape[1])))
    far_right = lax.ppermute(near_right, "y_hi", SWAP)
    far_rows = lax.ppermute(jnp.concatenate([sent_rows, lists]), "y_hi", SWAP)
    before = lax.ppermute(block, "z", UP)
    after = lax.ppermute(block, "z", DOWN)
    side = along_x(block, UP)
    across_low = lax.ppermute(before[:half], "z", UP)
    across_high = lax.ppermute(after[half:], "z", DOWN)
    side_before = along_x(before, UP)
    side_after = along_x(after, DOWN)
    corner_low = along_x(across_low, UP)
    corner_high = along_x(across_high, DOWN)
    early = (block, before, after, across_low, across_high, side, side_before, side_after)
    held = lax.optimization_barrier(early + (near_right, near_rows))
    mate_early = [to_mate(part) for part in held]
    late = (corner_low, corner_high, far_right, far_rows)
    mate_late = [to_mate(part) for part in late]
    mate_meta = to_mate(lax.optimization_barrier((meta, held[6]))[0])
    mate_late, mate_early = lax.optimization_barrier((mate_late, mate_early))

    def listed(buffer):
        return lax.slice(buffer, (size, 0), (size + meta.shape[0], meta.shape[1])).astype(jnp.int32)

    metas = jnp.stack([meta, listed(lax.optimization_barrier((far_rows, mate_late[3]))[0]), mate_meta, listed(mate_late[3])])
    waves = early + (corner_low, corner_high) + tuple(mate_early[:8] + mate_late[:2])
    operators = (near_right, near_rows, mate_early[8], mate_early[9], far_right, far_rows, mate_late[2], mate_late[3])
    return waves + operators, metas


def body(
    wavefunction,
    left_ops,
    right_ops,
    sector_dims,
    coupling_source,
    coupling_target,
    coupling_operator,
):
    ops, width, _ = left_ops.shape
    sectors = 4 * RING
    meta = jnp.stack([coupling_source, coupling_target, coupling_operator])
    shared, metas = share(wavefunction[0], left_ops, right_ops, meta)
    y, core = lax.axis_index("y_hi"), lax.axis_index("core")
    owners = jnp.stack([2 * y + core, 2 * (1 - y) + core, 2 * y + 1 - core, 2 * (1 - y) + 1 - core])
    chosen = metas[:, 2] + ops * owners.astype(jnp.int32)[:, None]
    table, ends = plan_couplings(
        metas[:, 0].reshape(-1), metas[:, 1].reshape(-1), chosen.reshape(-1), sector_dims, width // 2
    )
    smem = pl.BlockSpec(memory_space=pltpu.SMEM)
    hbm = pl.BlockSpec(memory_space=pltpu.HBM)
    rows = width // GROUP
    partial = pl.pallas_call(
        couplings_kernel,
        out_shape=jax.ShapeDtypeStruct((LEVELS, sectors, SLICE, width), jnp.bfloat16),
        in_specs=[smem] * 3 + [hbm] * len(shared),
        out_specs=hbm,
        scratch_shapes=[
            pltpu.VMEM((ops * width, width), jnp.bfloat16),
            pltpu.VMEM((ops * GROUP * width, width), jnp.bfloat16),
            pltpu.VMEM((sectors, width, width), jnp.bfloat16),
            pltpu.VMEM((sectors, ops * width, width), jnp.bfloat16),
            pltpu.VMEM((sectors + 1, rows, width), jnp.float32),
            pltpu.VMEM((LEVELS, sectors, SLICE, width), jnp.bfloat16),
            pltpu.SemaphoreType.DMA((8,)),
            pltpu.SemaphoreType.DMA((sectors,)),
            pltpu.SemaphoreType.DMA((LEVELS,)),
        ],
        compiler_params=pltpu.CompilerParams(vmem_limit_bytes=56 * MIB),
        name="couplings",
    )(table, ends, sector_dims, *shared)
    got = lax.all_to_all(partial.reshape(-1, 2, SLICE, width), REDUCE, 0, 0, tiled=True)
    total = jnp.sum(got.astype(jnp.float32), axis=0).astype(jnp.bfloat16)
    spread = jnp.broadcast_to(total[None], (8,) + total.shape).reshape((16,) + total.shape[1:])
    whole = lax.all_to_all(spread, SPREAD, 0, 0, tiled=True)
    whole = whole.reshape(2, 2, 2, 2, SLICE, width).transpose(0, 2, 1, 3, 4, 5)
    return whole.reshape(1, width, width).astype(jnp.float32)


def solution(mesh):
    fine = Mesh(mesh.devices.reshape(SIZES), AXES)
    everyone = P(AXES)
    placed = (
        P(SECTOR, None, None),
        P(AXES, None, None),
        P(AXES, None, None),
        P(),
        everyone,
        everyone,
        everyone,
    )
    return jax.shard_map(
        body, mesh=fine, in_specs=placed, out_specs=P(SECTOR, None, None), check_vma=False
    )
```

```python
import jax
import jax.numpy as jnp
from jax import lax
from jax.experimental import pallas as pl
from jax.experimental.pallas import tpu as pltpu
from jax.sharding import Mesh, PartitionSpec as P

AXES = ("x_hi", "y_hi", "y_lo", "x_lo", "z", "core")
SIZES = (2, 2, 2, 2, 4, 2)
SECTOR = ("x_lo", "z", "core")
REDUCE = ("x_hi", "y_lo", "x_lo", "z")
SPREAD = ("x_hi", "y_hi", "y_lo", "core")
RING = 4
GROUP = 4
LEVELS = 4
GRAIN = 128
SLICE = GRAIN // GROUP
STEP = 8
KINDS = 4
AHEAD = 4
MIB = 1024 * 1024
SWAP = [(0, 1), (1, 0)]
UP = [(i, (i + 1) % RING) for i in range(RING)]
DOWN = [(i, (i - 1) % RING) for i in range(RING)]
SHIFTS = (0, RING - 1, 1, 2)


def plan_couplings(source, target, op, dims, half):
    sectors = dims.shape[0]
    count = source.shape[0]
    steps = (count + KINDS * (STEP - 1)) // STEP
    index = jnp.arange(sectors, dtype=jnp.int32)[None, :]
    wide = (dims > half).astype(jnp.int32)[None, :]
    wide_source = jnp.sum(jnp.where(source[:, None] == index, wide, 0), axis=1)
    wide_target = jnp.sum(jnp.where(target[:, None] == index, wide, 0), axis=1)
    kind = 2 * wide_source + wide_target
    kinds = jnp.arange(KINDS, dtype=jnp.int32)
    is_kind = kind[:, None] == kinds[None, :]
    taken = (jnp.sum(is_kind.astype(jnp.int32), axis=0) + STEP - 1) // STEP
    end = jnp.sum(jnp.where(kinds[:, None] <= kinds[None, :], taken[:, None], 0), axis=0)
    start = end - taken
    spot = jnp.arange(count, dtype=jnp.int32)
    earlier = (kind[:, None] == kind[None, :]) & (spot[:, None] < spot[None, :])
    rank = jnp.sum(earlier.astype(jnp.int32), axis=0)
    place = rank + STEP * jnp.sum(jnp.where(is_kind, start[None, :], 0), axis=1)
    here = place[:, None] == jnp.arange(steps * STEP, dtype=jnp.int32)[None, :]
    code = (op * sectors + source) * (2 * sectors) + target - sectors
    return sectors + jnp.sum(jnp.where(here, code[:, None], 0), axis=0), end


def couplings_kernel(table, ends, dims, *refs):
    own_waves, mate_waves = refs[:10], refs[10:20]
    own_right, own_left, mate_right, mate_left, far_right, far_left, far_mate_right, far_mate_left = refs[20:28]
    out, left, right, waves, halves, sums, rounded, op_sems, wave_sems, out_sems = refs[28:]
    y, x, z, core = (lax.axis_index(name) for name in ("y_hi", "x_lo", "z", "core"))
    sectors, width, _ = waves.shape
    rows = sums.shape[1]
    ops = own_right.shape[0] // width
    half = width // 2
    left_copies, right_copies = [], []
    for n, (pair, c, left_rows, right_ops) in enumerate((
        (y, core, own_left, own_right),
        (y, 1 - core, mate_left, mate_right),
        (1 - y, core, far_left, far_right),
        (1 - y, 1 - core, far_mate_left, far_mate_right),
    )):
        first = (pair * 2 + c) * ops
        size = ops * rows
        part = left_rows.at[pl.ds(pl.multiple_of(core * size, size), size)]
        to = left.at[pl.ds(pl.multiple_of(first * rows, size), size)]
        left_copies.append(pltpu.make_async_copy(part, to, op_sems.at[2 * n]))
        to = right.at[pl.ds(pl.multiple_of(first * width, ops * width), ops * width)]
        right_copies.append(pltpu.make_async_copy(right_ops, to, op_sems.at[2 * n + 1]))
    for copy in left_copies:
        copy.start()
    whole, low, high = (pl.ds(0, width), pl.ds(0, half), pl.ds(half, half))
    places = (
        (0, whole), (1, whole), (2, whole), (3, low), (3, high),
        (4, whole), (5, whole), (6, whole), (7, low), (7, high),
    )
    wave_copies = [[] for _ in range(sectors)]
    for c, pieces in ((0, own_waves), (1, mate_waves)):
        for piece, (place, part) in zip(pieces, places):
            slot = c * (sectors // 2) + place
            wave_copies[slot].append(pltpu.make_async_copy(piece, waves.at[slot, part], wave_sems.at[slot]))
    for slot in range(AHEAD):
        for copy in wave_copies[slot]:
            copy.start()
    sums[...] = jnp.zeros_like(sums)
    for copy in left_copies:
        copy.wait()

    def first_half(slot, carry):
        for later in range(AHEAD, sectors):

            @pl.when(slot == later - AHEAD)
            def _(later=later):
                for copy in wave_copies[later]:
                    copy.start()

        @pl.when(slot == sectors - AHEAD)
        def _():
            for copy in right_copies:
                copy.start()

        pltpu.make_async_copy(waves.at[slot], waves.at[slot], wave_sems.at[slot]).wait()
        other_core = lax.div(slot, sectors // 2)
        other_x = lax.rem(lax.div(slot, RING), 2)
        step = lax.rem(slot, RING)
        shift = jnp.where(step == 1, RING - 1, jnp.where(step == 2, 1, jnp.where(step == 3, 2, 0)))
        x_at = lax.rem(x + other_x, 2)
        core_at = lax.rem(core + other_core, 2)
        s = (x_at * RING + lax.rem(z + shift, RING)) * 2 + core_at
        level = dims[s] // GRAIN
        for sl in range(1, LEVELS + 1):

            @pl.when(level == sl)
            def _(sl=sl):
                inner = sl * GRAIN
                halves[s, :, :inner] = jnp.dot(
                    left[:, :inner], waves[slot, :inner, :inner], preferred_element_type=jnp.float32
                ).astype(jnp.bfloat16)
                if sl % 2:
                    halves[s, :, inner:inner + GRAIN] = jnp.zeros((left.shape[0], GRAIN), jnp.bfloat16)

        return carry

    lax.fori_loop(0, sectors, first_half, 0)
    for copy in right_copies:
        copy.wait()

    for kind in range(KINDS):
        inner = width if kind >= 2 else half
        cols = width if kind % 2 else half
        used = rows if kind % 2 else rows // 2

        def second_half(i, carry, inner=inner, cols=cols, used=used):
            for u in range(STEP):
                code = table[i * STEP + u]
                target = jnp.bitwise_and(code, 2 * sectors - 1)
                source = jnp.bitwise_and(lax.shift_right_logical(code, 5), sectors - 1)
                op = lax.shift_right_logical(code, 9)
                block = halves[source, pl.ds(pl.multiple_of(op * rows, rows), used), :inner]
                sums[target, :used, :cols] += jnp.dot(
                    block,
                    right[pl.ds(pl.multiple_of(op * width, width), inner), :cols],
                    preferred_element_type=jnp.float32,
                )
            return carry

        lax.fori_loop(0 if kind == 0 else ends[kind - 1], ends[kind], second_half, 0)
    parts = out.shape[0]
    size = rows // parts
    column = lax.broadcasted_iota(jnp.int32, (size, width), 1)
    copies = []
    for part in range(parts):

        def finish(s, carry, part=part):
            limit = jnp.where(dims[s] > part * GRAIN, dims[s], 0)
            total = jnp.where(column < limit, sums[s, part * size:(part + 1) * size, :], 0.0)
            rounded[part, s] = total.astype(jnp.bfloat16)
            return carry

        lax.fori_loop(0, sectors, finish, 0)
        copy = pltpu.make_async_copy(rounded.at[part], out.at[part], out_sems.at[part])
        copy.start()
        copies.append(copy)
    for copy in copies:
        copy.wait()


def along_x(part, steps):
    return lax.ppermute(part, ("x_hi", "x_lo"), steps)


def to_mate(part):
    return lax.ppermute(part, "core", SWAP)


def share(block, left_ops, right_ops, meta):
    ops, width, _ = left_ops.shape
    half = width // 2
    size = ops * LEVELS * SLICE * 2
    rows = left_ops.reshape(ops, LEVELS, 2, 2, SLICE, width).transpose(2, 3, 0, 1, 4, 5)
    rows = rows.reshape(2, size, width)
    y = lax.axis_index("y_hi")
    near_rows = lax.dynamic_index_in_dim(rows, y, 0, keepdims=False)
    sent_rows = lax.dynamic_index_in_dim(rows, 1 - y, 0, keepdims=False)
    near_right = right_ops.reshape(ops * width, width)
    lists = jnp.pad(meta.astype(jnp.bfloat16), ((0, 16 - meta.shape[0]), (0, width - meta.shape[1])))
    near_rows = jnp.concatenate([near_rows, lists])
    far_right = lax.ppermute(near_right, "y_hi", SWAP)
    far_rows = lax.ppermute(jnp.concatenate([sent_rows, lists]), "y_hi", SWAP)
    before = lax.ppermute(block, "z", UP)
    after = lax.ppermute(block, "z", DOWN)
    side = along_x(block, UP)
    across_low = lax.ppermute(before[:half], "z", UP)
    across_high = lax.ppermute(after[half:], "z", DOWN)
    side_before = along_x(before, UP)
    side_after = along_x(after, DOWN)
    corner_low = along_x(across_low, UP)
    corner_high = along_x(across_high, DOWN)
    early = (block, before, after, across_low, across_high, side, side_before, side_after)
    held = lax.optimization_barrier(early + (near_right, near_rows))
    mate_early = [to_mate(part) for part in held]
    late = (corner_low, corner_high, far_right, far_rows)
    mate_late = [to_mate(part) for part in late]
    mate_late, mate_early = lax.optimization_barrier((mate_late, mate_early))

    def listed(buffer):
        return lax.slice(buffer, (size, 0), (size + meta.shape[0], meta.shape[1])).astype(jnp.int32)

    metas = jnp.stack([meta, listed(lax.optimization_barrier((far_rows, mate_late[3]))[0]), listed(mate_early[9]), listed(mate_late[3])])
    waves = early + (corner_low, corner_high) + tuple(mate_early[:8] + mate_late[:2])
    operators = (near_right, near_rows, mate_early[8], mate_early[9], far_right, far_rows, mate_late[2], mate_late[3])
    return waves + operators, metas


def body(
    wavefunction,
    left_ops,
    right_ops,
    sector_dims,
    coupling_source,
    coupling_target,
    coupling_operator,
):
    ops, width, _ = left_ops.shape
    sectors = 4 * RING
    meta = jnp.stack([coupling_source, coupling_target, coupling_operator])
    shared, metas = share(wavefunction[0], left_ops, right_ops, meta)
    y, core = lax.axis_index("y_hi"), lax.axis_index("core")
    owners = jnp.stack([2 * y + core, 2 * (1 - y) + core, 2 * y + 1 - core, 2 * (1 - y) + 1 - core])
    chosen = metas[:, 2] + ops * owners.astype(jnp.int32)[:, None]
    table, ends = plan_couplings(
        metas[:, 0].reshape(-1), metas[:, 1].reshape(-1), chosen.reshape(-1), sector_dims, width // 2
    )
    smem = pl.BlockSpec(memory_space=pltpu.SMEM)
    hbm = pl.BlockSpec(memory_space=pltpu.HBM)
    rows = width // GROUP
    partial = pl.pallas_call(
        couplings_kernel,
        out_shape=jax.ShapeDtypeStruct((LEVELS, sectors, SLICE, width), jnp.bfloat16),
        in_specs=[smem] * 3 + [hbm] * len(shared),
        out_specs=hbm,
        scratch_shapes=[
            pltpu.VMEM((ops * width, width), jnp.bfloat16),
            pltpu.VMEM((ops * GROUP * width, width), jnp.bfloat16),
            pltpu.VMEM((sectors, width, width), jnp.bfloat16),
            pltpu.VMEM((sectors, ops * width, width), jnp.bfloat16),
            pltpu.VMEM((sectors + 1, rows, width), jnp.float32),
            pltpu.VMEM((LEVELS, sectors, SLICE, width), jnp.bfloat16),
            pltpu.SemaphoreType.DMA((8,)),
            pltpu.SemaphoreType.DMA((sectors,)),
            pltpu.SemaphoreType.DMA((LEVELS,)),
        ],
        compiler_params=pltpu.CompilerParams(vmem_limit_bytes=56 * MIB),
        name="couplings",
    )(table, ends, sector_dims, *shared)
    got = lax.all_to_all(partial.reshape(-1, 2, SLICE, width), REDUCE, 0, 0, tiled=True)
    total = jnp.sum(got.astype(jnp.float32), axis=0).astype(jnp.bfloat16)
    spread = jnp.broadcast_to(total[None], (8,) + total.shape).reshape((16,) + total.shape[1:])
    whole = lax.all_to_all(spread, SPREAD, 0, 0, tiled=True)
    whole = whole.reshape(2, 2, 2, 2, SLICE, width).transpose(0, 2, 1, 3, 4, 5)
    return whole.reshape(1, width, width).astype(jnp.float32)


def solution(mesh):
    fine = Mesh(mesh.devices.reshape(SIZES), AXES)
    everyone = P(AXES)
    placed = (
        P(SECTOR, None, None),
        P(AXES, None, None),
        P(AXES, None, None),
        P(),
        everyone,
        everyone,
        everyone,
    )
    return jax.shard_map(
        body, mesh=fine, in_specs=placed, out_specs=P(SECTOR, None, None), check_vma=False
    )
```

```python
import jax
import jax.numpy as jnp
from jax import lax
from jax.experimental import pallas as pl
from jax.experimental.pallas import tpu as pltpu
from jax.sharding import Mesh, PartitionSpec as P

AXES = ("x_hi", "y_hi", "y_lo", "x_lo", "z", "core")
SIZES = (2, 2, 2, 2, 4, 2)
SECTOR = ("x_lo", "z", "core")
REDUCE = ("x_hi", "y_lo", "x_lo", "z")
SPREAD = ("x_hi", "y_hi", "y_lo", "core")
RING = 4
GROUP = 4
LEVELS = 4
GRAIN = 128
SLICE = GRAIN // GROUP
STEP = 8
KINDS = 4
AHEAD = 4
MIB = 1024 * 1024
SWAP = [(0, 1), (1, 0)]
UP = [(i, (i + 1) % RING) for i in range(RING)]
DOWN = [(i, (i - 1) % RING) for i in range(RING)]
SHIFTS = (0, RING - 1, 1, 2)


def plan_couplings(source, target, op, dims, half):
    sectors = dims.shape[0]
    count = source.shape[0]
    steps = (count + KINDS * (STEP - 1)) // STEP
    index = jnp.arange(sectors, dtype=jnp.int32)[None, :]
    wide = (dims > half).astype(jnp.int32)[None, :]
    wide_source = jnp.sum(jnp.where(source[:, None] == index, wide, 0), axis=1)
    wide_target = jnp.sum(jnp.where(target[:, None] == index, wide, 0), axis=1)
    kind = 2 * wide_source + wide_target
    kinds = jnp.arange(KINDS, dtype=jnp.int32)
    is_kind = kind[:, None] == kinds[None, :]
    taken = (jnp.sum(is_kind.astype(jnp.int32), axis=0) + STEP - 1) // STEP
    end = jnp.sum(jnp.where(kinds[:, None] <= kinds[None, :], taken[:, None], 0), axis=0)
    start = end - taken
    spot = jnp.arange(count, dtype=jnp.int32)
    earlier = (kind[:, None] == kind[None, :]) & (spot[:, None] < spot[None, :])
    rank = jnp.sum(earlier.astype(jnp.int32), axis=0)
    place = rank + STEP * jnp.sum(jnp.where(is_kind, start[None, :], 0), axis=1)
    here = place[:, None] == jnp.arange(steps * STEP, dtype=jnp.int32)[None, :]
    code = (op * sectors + source) * (2 * sectors) + target - sectors
    return sectors + jnp.sum(jnp.where(here, code[:, None], 0), axis=0), end


def couplings_kernel(table, ends, dims, *refs):
    own_waves, mate_waves = refs[:10], refs[10:20]
    own_right, own_left, mate_right, mate_left, far_right, far_left, far_mate_right, far_mate_left = refs[20:28]
    out, left, right, waves, halves, sums, rounded, op_sems, wave_sems, out_sems = refs[28:]
    y, x, z, core = (lax.axis_index(name) for name in ("y_hi", "x_lo", "z", "core"))
    sectors, width, _ = waves.shape
    rows = sums.shape[1]
    ops = own_right.shape[0] // width
    half = width // 2
    left_copies, right_copies = [], []
    for n, (pair, c, left_rows, right_ops) in enumerate((
        (y, core, own_left, own_right),
        (y, 1 - core, mate_left, mate_right),
        (1 - y, core, far_left, far_right),
        (1 - y, 1 - core, far_mate_left, far_mate_right),
    )):
        first = (pair * 2 + c) * ops
        size = ops * rows
        part = left_rows.at[pl.ds(pl.multiple_of(core * size, size), size)]
        to = left.at[pl.ds(pl.multiple_of(first * rows, size), size)]
        left_copies.append(pltpu.make_async_copy(part, to, op_sems.at[2 * n]))
        to = right.at[pl.ds(pl.multiple_of(first * width, ops * width), ops * width)]
        right_copies.append(pltpu.make_async_copy(right_ops, to, op_sems.at[2 * n + 1]))
    for copy in left_copies:
        copy.start()
    whole, low, high = (pl.ds(0, width), pl.ds(0, half), pl.ds(half, half))
    places = (
        (0, whole), (1, whole), (2, whole), (3, low), (3, high),
        (4, whole), (5, whole), (6, whole), (7, low), (7, high),
    )
    wave_copies = [[] for _ in range(sectors)]
    for c, pieces in ((0, own_waves), (1, mate_waves)):
        for piece, (place, part) in zip(pieces, places):
            slot = c * (sectors // 2) + place
            wave_copies[slot].append(pltpu.make_async_copy(piece, waves.at[slot, part], wave_sems.at[slot]))
    for slot in range(AHEAD):
        for copy in wave_copies[slot]:
            copy.start()
    sums[...] = jnp.zeros_like(sums)
    for copy in left_copies:
        copy.wait()

    def first_half(slot, carry):
        for later in range(AHEAD, sectors):

            @pl.when(slot == later - AHEAD)
            def _(later=later):
                for copy in wave_copies[later]:
                    copy.start()

        @pl.when(slot == sectors - AHEAD)
        def _():
            for copy in right_copies:
                copy.start()

        pltpu.make_async_copy(waves.at[slot], waves.at[slot], wave_sems.at[slot]).wait()
        other_core = lax.div(slot, sectors // 2)
        other_x = lax.rem(lax.div(slot, RING), 2)
        step = lax.rem(slot, RING)
        shift = jnp.where(step == 1, RING - 1, jnp.where(step == 2, 1, jnp.where(step == 3, 2, 0)))
        x_at = lax.rem(x + other_x, 2)
        core_at = lax.rem(core + other_core, 2)
        s = (x_at * RING + lax.rem(z + shift, RING)) * 2 + core_at
        level = dims[s] // GRAIN
        for sl in range(1, LEVELS + 1):

            @pl.when(level == sl)
            def _(sl=sl):
                inner = sl * GRAIN
                halves[s, :, :inner] = jnp.dot(
                    left[:, :inner], waves[slot, :inner, :inner], preferred_element_type=jnp.float32
                ).astype(jnp.bfloat16)
                if sl % 2:
                    halves[s, :, inner:inner + GRAIN] = jnp.zeros((left.shape[0], GRAIN), jnp.bfloat16)

        return carry

    lax.fori_loop(0, sectors, first_half, 0)
    for copy in right_copies:
        copy.wait()

    for kind in range(KINDS):
        inner = width if kind >= 2 else half
        cols = width if kind % 2 else half
        used = rows if kind % 2 else rows // 2

        def second_half(i, carry, inner=inner, cols=cols, used=used):
            for u in range(STEP):
                code = table[i * STEP + u]
                target = jnp.bitwise_and(code, 2 * sectors - 1)
                source = jnp.bitwise_and(lax.shift_right_logical(code, 5), sectors - 1)
                op = lax.shift_right_logical(code, 9)
                block = halves[source, pl.ds(pl.multiple_of(op * rows, rows), used), :inner]
                sums[target, :used, :cols] += jnp.dot(
                    block,
                    right[pl.ds(pl.multiple_of(op * width, width), inner), :cols],
                    preferred_element_type=jnp.float32,
                )
            return carry

        lax.fori_loop(0 if kind == 0 else ends[kind - 1], ends[kind], second_half, 0)
    parts = out.shape[0]
    size = rows // parts
    column = lax.broadcasted_iota(jnp.int32, (size, width), 1)
    copies = []
    for part in range(parts):

        def finish(s, carry, part=part):
            limit = jnp.where(dims[s] > part * GRAIN, dims[s], 0)
            total = jnp.where(column < limit, sums[s, part * size:(part + 1) * size, :], 0.0)
            rounded[part, s] = total.astype(jnp.bfloat16)
            return carry

        lax.fori_loop(0, sectors, finish, 0, unroll=True)
        copy = pltpu.make_async_copy(rounded.at[part], out.at[part], out_sems.at[part])
        copy.start()
        copies.append(copy)
    for copy in copies:
        copy.wait()


def along_x(part, steps):
    return lax.ppermute(part, ("x_hi", "x_lo"), steps)


def to_mate(part):
    return lax.ppermute(part, "core", SWAP)


def share(block, left_ops, right_ops, meta):
    ops, width, _ = left_ops.shape
    half = width // 2
    size = ops * LEVELS * SLICE * 2
    rows = left_ops.reshape(ops, LEVELS, 2, 2, SLICE, width).transpose(2, 3, 0, 1, 4, 5)
    rows = rows.reshape(2, size, width)
    y = lax.axis_index("y_hi")
    near_rows = lax.dynamic_index_in_dim(rows, y, 0, keepdims=False)
    sent_rows = lax.dynamic_index_in_dim(rows, 1 - y, 0, keepdims=False)
    near_right = right_ops.reshape(ops * width, width)
    lists = jnp.pad(meta.astype(jnp.bfloat16), ((0, 16 - meta.shape[0]), (0, width - meta.shape[1])))
    near_rows = jnp.concatenate([near_rows, lists])
    far_right = lax.ppermute(near_right, "y_hi", SWAP)
    far_rows = lax.ppermute(jnp.concatenate([sent_rows, lists]), "y_hi", SWAP)
    before = lax.ppermute(block, "z", UP)
    after = lax.ppermute(block, "z", DOWN)
    side = along_x(block, UP)
    across_low = lax.ppermute(before[:half], "z", UP)
    across_high = lax.ppermute(after[half:], "z", DOWN)
    side_before = along_x(before, UP)
    side_after = along_x(after, DOWN)
    corner_low = along_x(across_low, UP)
    corner_high = along_x(across_high, DOWN)
    early = (block, before, after, across_low, across_high, side, side_before, side_after)
    held = lax.optimization_barrier(early + (near_right, near_rows))
    mate_early = [to_mate(part) for part in held]
    late = (corner_low, corner_high, far_right, far_rows)
    mate_late = [to_mate(part) for part in late]
    mate_late, mate_early = lax.optimization_barrier((mate_late, mate_early))

    def listed(buffer):
        return lax.slice(buffer, (size, 0), (size + meta.shape[0], meta.shape[1])).astype(jnp.int32)

    metas = jnp.stack([meta, listed(lax.optimization_barrier((far_rows, mate_late[3]))[0]), listed(mate_early[9]), listed(mate_late[3])])
    waves = early + (corner_low, corner_high) + tuple(mate_early[:8] + mate_late[:2])
    operators = (near_right, near_rows, mate_early[8], mate_early[9], far_right, far_rows, mate_late[2], mate_late[3])
    return waves + operators, metas


def body(
    wavefunction,
    left_ops,
    right_ops,
    sector_dims,
    coupling_source,
    coupling_target,
    coupling_operator,
):
    ops, width, _ = left_ops.shape
    sectors = 4 * RING
    meta = jnp.stack([coupling_source, coupling_target, coupling_operator])
    shared, metas = share(wavefunction[0], left_ops, right_ops, meta)
    y, core = lax.axis_index("y_hi"), lax.axis_index("core")
    owners = jnp.stack([2 * y + core, 2 * (1 - y) + core, 2 * y + 1 - core, 2 * (1 - y) + 1 - core])
    chosen = metas[:, 2] + ops * owners.astype(jnp.int32)[:, None]
    table, ends = plan_couplings(
        metas[:, 0].reshape(-1), metas[:, 1].reshape(-1), chosen.reshape(-1), sector_dims, width // 2
    )
    smem = pl.BlockSpec(memory_space=pltpu.SMEM)
    hbm = pl.BlockSpec(memory_space=pltpu.HBM)
    rows = width // GROUP
    partial = pl.pallas_call(
        couplings_kernel,
        out_shape=jax.ShapeDtypeStruct((LEVELS, sectors, SLICE, width), jnp.bfloat16),
        in_specs=[smem] * 3 + [hbm] * len(shared),
        out_specs=hbm,
        scratch_shapes=[
            pltpu.VMEM((ops * width, width), jnp.bfloat16),
            pltpu.VMEM((ops * GROUP * width, width), jnp.bfloat16),
            pltpu.VMEM((sectors, width, width), jnp.bfloat16),
            pltpu.VMEM((sectors, ops * width, width), jnp.bfloat16),
            pltpu.VMEM((sectors + 1, rows, width), jnp.float32),
            pltpu.VMEM((LEVELS, sectors, SLICE, width), jnp.bfloat16),
            pltpu.SemaphoreType.DMA((8,)),
            pltpu.SemaphoreType.DMA((sectors,)),
            pltpu.SemaphoreType.DMA((LEVELS,)),
        ],
        compiler_params=pltpu.CompilerParams(vmem_limit_bytes=56 * MIB),
        name="couplings",
    )(table, ends, sector_dims, *shared)
    got = lax.all_to_all(partial.reshape(-1, 2, SLICE, width), REDUCE, 0, 0, tiled=True)
    total = jnp.sum(got.astype(jnp.float32), axis=0).astype(jnp.bfloat16)
    spread = jnp.broadcast_to(total[None], (8,) + total.shape).reshape((16,) + total.shape[1:])
    whole = lax.all_to_all(spread, SPREAD, 0, 0, tiled=True)
    whole = whole.reshape(2, 2, 2, 2, SLICE, width).transpose(0, 2, 1, 3, 4, 5)
    return whole.reshape(1, width, width).astype(jnp.float32)


def solution(mesh):
    fine = Mesh(mesh.devices.reshape(SIZES), AXES)
    everyone = P(AXES)
    placed = (
        P(SECTOR, None, None),
        P(AXES, None, None),
        P(AXES, None, None),
        P(),
        everyone,
        everyone,
        everyone,
    )
    return jax.shard_map(
        body, mesh=fine, in_specs=placed, out_specs=P(SECTOR, None, None), check_vma=False
    )
```
